512 devices in a mesh: gx: 32 (over x, y, core), gy: 16 (over z).
Axes of the slice: x: 4, y: 4, z: 16, core: 2. Of those that a mesh axis runs over, the one named last changes fastest.
Arguments:
- queries: bfloat16 [16384, 256], P(('gx', 'gy')), may hold values from -32 to 32
- positions: int32 [16384], P(('gx', 'gy')), may hold values from 0 to 65535
- queue: bfloat16 [65536, 256], P('gx'), may hold values from -4 to 4
- new_keys: bfloat16 [2048, 256], P(('gx', 'gy')), may hold values from -4 to 4
- step: int32 [1], replicated, may hold values from 0 to 1023
Outputs:
- losses: float32 [16384], P(('gx', 'gy'))
- query_grad: bfloat16 [16384, 256], P(('gx', 'gy'))
- updated_queue: bfloat16 [65536, 256], P('gx')
The draws below stay inside these ranges and needn't reach their ends.
All inputs are finite; a program needn't handle non-finite values.
Results may differ from the reference program's by a relative error of at most 0.0029.
Values may be sent and summed in bfloat16 or wider, within the bound.
No kernel may reach another device: no remote copies, remote signals or barrier semaphores. Data moves between devices by JAX's collectives and lax.ppermute only.
A program may use at most 64 MiB of HBM per device.

```python
import math
import jax
import jax.numpy as jnp
from jax import lax

E = 256
KEY_DEV = 2048
BATCH = 16384
QUEUE = 65536
N_GX = 32


def queue_base(key):
    base = jnp.clip(jax.random.normal(jax.random.fold_in(key, 11), (QUEUE, E), jnp.float32), -4.0, 4.0)
    pairs = base.reshape(QUEUE // 2, 2, E)
    second = pairs[:, 1]
    joined = jnp.stack([pairs[:, 0], second], axis=1).reshape(QUEUE, E)
    return jnp.clip(joined, -4.0, 4.0)


def draw_queue(key, part):
    table = queue_base(key)
    return table.astype(jnp.bfloat16)


def draw_queries(key, part):
    key = jax.random.fold_in(key, 3)
    rows = jnp.clip(jax.random.normal(key, (BATCH, E), jnp.float32), -4.0, 4.0)
    return rows.astype(jnp.bfloat16)


def plant(entries, stream_key, least, top_value):
    spot = [jax.random.randint(jax.random.fold_in(stream_key, axis), (), 0, length) for axis, length in enumerate(entries.shape)]
    main_axis = entries.shape.index(max(entries.shape))
    next_to = spot[:main_axis] + [(spot[main_axis] + 1) % entries.shape[main_axis]] + spot[main_axis + 1:]
    return entries.at[tuple(spot)].set(least).at[tuple(next_to)].set(top_value)


def steps_of(rng, extent, cuts, low, top_value):
    loudness = 1.0
    for dim, blocks in cuts:
        heights = jax.random.uniform(jax.random.fold_in(jax.random.fold_in(rng, 6), dim), (blocks,), jnp.float32, low / len(cuts), top_value / len(cuts))
        loudness = loudness * jnp.repeat(jnp.exp(heights), extent[dim] // blocks).reshape((-1,) + (1,) * (len(extent) - 1 - dim))
    return loudness


def bell_draw(rng, dims, width, bound, shards=(), held_as=jnp.bfloat16):
    gain = steps_of(rng, dims, shards, -0.22, 0.18) if shards else 1.0
    result = jax.random.normal(rng, dims, jnp.float32) * width * gain
    return jnp.minimum(jnp.maximum(result, -bound), bound).astype(held_as)


def setup_inputs(seed: int = 0) -> dict:
    seeds = jax.random.split(jax.random.key(seed), 6)
    return {
        "queries": draw_queries(jax.random.fold_in(seeds[5], 71), 0),
        "positions": plant(jax.random.randint(seeds[1], (BATCH,), 0, QUEUE), jax.random.fold_in(seeds[1], 1), 0, QUEUE - 1).astype(jnp.int32),
        "queue": draw_queue(jax.random.fold_in(seeds[5], 71), 0),
        "new_keys": bell_draw(seeds[3], (KEY_DEV, E), 1.0, 4.0, ((0, 512),)),
        "step": jax.random.randint(seeds[4], (1,), 0, 1024).astype(jnp.int32),
    }


def reference(queries, positions, queue, new_keys, step):
    scale = 2.0 / math.sqrt(E)
    block = math.gcd(BATCH, 256)
    query_blocks = queries.reshape(BATCH // block, block, E)
    pos_blocks = positions.reshape(BATCH // block, block)

    def one_block(pair):
        rows, targets = pair
        scores = jnp.dot(rows, queue.T, preferred_element_type=jnp.float32) * scale
        top = lax.optimization_barrier(jnp.max(scores, axis=1))
        lse = top + jnp.log(lax.optimization_barrier(jnp.sum(jnp.exp(scores - top[:, None]), axis=1)))
        hits = lax.broadcasted_iota(jnp.int32, scores.shape, 1) == targets[:, None]
        positive = lax.optimization_barrier(jnp.sum(jnp.where(hits, scores, 0.0), axis=1))
        weights = (jnp.exp(scores - lse[:, None]) - hits.astype(scores.dtype)).astype(jnp.bfloat16)
        grad = (jnp.dot(weights, queue, preferred_element_type=jnp.float32) * scale).astype(jnp.bfloat16)
        return (lse - positive, grad)
    losses, grads = lax.map(one_block, (query_blocks, pos_blocks))
    owner = step[0] % N_GX
    slabs = queue.reshape(N_GX, KEY_DEV, E)
    chosen = jnp.arange(N_GX, dtype=jnp.int32) == owner
    updated = jnp.where(chosen[:, None, None], new_keys[None], slabs).reshape(QUEUE, E)
    return (losses.reshape(BATCH), grads.reshape(BATCH, E), updated)
```

```python
import math

import jax
import jax.numpy as jnp
import numpy as np
from jax import lax
from jax.experimental import pallas as pl
from jax.experimental.pallas import tpu as pltpu
from jax.sharding import Mesh, PartitionSpec as P

BF = jnp.bfloat16
F32 = jnp.float32
ROWS = 48
LOG2E = 1.4426950408889634
VMEM = pl.BlockSpec(memory_space=pltpu.VMEM)
SMEM = pl.BlockSpec(memory_space=pltpu.SMEM)


def rows_dot(a, b):
    return lax.dot_general(a, b, (((1,), (1,)), ((), ())), preferred_element_type=F32)


def partial_kernel(scale, srcs, nq, first_ref, msg_ref, own_ref, other_ref, out_ref, q_ref, s_ref):
    width = own_ref.shape[1]
    slab = own_ref.shape[0]
    n = srcs * nq
    block = 512
    lane = lax.broadcasted_iota(jnp.int32, (nq, width), 1)
    row = lax.broadcasted_iota(jnp.int32, (nq, width), 0)
    parts = []
    for j in range(srcs):
        q_ref[j * nq:(j + 1) * nq, :] = msg_ref[j, :nq, :]
        tail = msg_ref[j, nq:, :].astype(F32)
        line = jnp.broadcast_to(tail[4:5, :], (nq, width))
        hi = jnp.sum(jnp.where(lane == row, line, 0.0), axis=1, keepdims=True)
        lo = jnp.sum(jnp.where(lane == row + nq, line, 0.0), axis=1, keepdims=True)
        parts.append(hi * 256.0 + lo)
    target = jnp.concatenate(parts, axis=0).astype(jnp.int32)
    queries = q_ref[...]
    top = None
    blocks = []
    for half, ref in enumerate((own_ref, other_ref)):
        for b in range(slab // block):
            blocks.append((half, ref, b))
    for i, (half, ref, b) in enumerate(blocks):
        s = rows_dot(queries, ref[b * block:(b + 1) * block, :])
        s_ref[:, i * block:(i + 1) * block] = s
        for c in range(block // 128):
            piece = s[:, c * 128:(c + 1) * 128]
            top = piece if top is None else jnp.maximum(top, piece)
    point = jnp.max(top, axis=1, keepdims=True).astype(BF).astype(F32)
    total = jnp.zeros((n, 128), F32)
    grad = jnp.zeros((n, width), F32)
    positive = jnp.zeros((n, width), F32)
    column = lax.broadcasted_iota(jnp.int32, (n, block), 1)
    for i, (half, ref, b) in enumerate(blocks):
        s = s_ref[:, i * block:(i + 1) * block]
        hit = column == (target - (first_ref[half] + b * block))
        e = jnp.where(hit, 0.0, jnp.exp2((s - point) * (scale * LOG2E)))
        for c in range(block // 128):
            total += e[:, c * 128:(c + 1) * 128]
        keys = ref[b * block:(b + 1) * block, :]
        grad += jnp.dot(e.astype(BF), keys, preferred_element_type=F32)
        positive += jnp.dot(hit.astype(F32).astype(BF), keys, preferred_element_type=F32)
    total = jnp.sum(total, axis=1, keepdims=True)
    t0 = total.astype(BF).astype(F32)
    t1 = (total - t0).astype(BF).astype(F32)
    t2 = total - t0 - t1
    place = lax.broadcasted_iota(jnp.int32, (n, 128), 1)
    stats = jnp.where(place == 0, point, jnp.where(place == 1, t0, jnp.where(place == 2, t1, jnp.where(place == 3, t2, 0.0))))
    stats = stats.astype(BF)
    grad = grad.astype(BF)
    positive = positive.astype(BF)
    for j in range(srcs):
        at = slice(j * nq, (j + 1) * nq)
        out_ref[j, :, :width] = grad[at]
        out_ref[j, :, width:2 * width] = positive[at]
        out_ref[j, :, 2 * width:] = stats[at]


def combine_kernel(scale, srcs, nq, got_ref, q_ref, loss_ref, grad_ref):
    width = q_ref.shape[1]
    positive = jnp.zeros((nq, width), F32)
    points, totals = [], []
    for j in range(srcs):
        positive += got_ref[j, :, width:2 * width].astype(F32)
        st = got_ref[j, :, 2 * width:].astype(F32)
        points.append(st[:, 0:1])
        totals.append(st[:, 1:2] + st[:, 2:3] + st[:, 3:4])
    s_pos = jnp.sum(q_ref[...].astype(F32) * positive, axis=1, keepdims=True)
    top = s_pos
    for p in points:
        top = jnp.maximum(top, p)
    total = jnp.exp2((s_pos - top) * (scale * LOG2E))
    grad = jnp.zeros((nq, width), F32)
    for j in range(srcs):
        a = jnp.exp2((points[j] - top) * (scale * LOG2E))
        total += a * totals[j]
        grad += a * got_ref[j, :, :width].astype(F32)
    log_total = jnp.log(total)
    lse = top * scale + log_total
    weight = (jnp.exp(s_pos * scale - lse) - 1.0).astype(BF).astype(F32)
    grad_ref[...] = ((grad / total + weight * positive) * scale).astype(BF)
    loss = lse - s_pos * scale
    lane = lax.broadcasted_iota(jnp.int32, (nq, 128), 1)
    row = lax.broadcasted_iota(jnp.int32, (nq, 128), 0)
    loss_ref[...] = jnp.sum(jnp.where(lane == row, loss, 0.0), axis=0, keepdims=True)


def local(queries, positions, queue, new_keys, step):
    nq, width = queries.shape
    slab = queue.shape[0]
    nk = new_keys.shape[0]
    nz = lax.axis_size("z")
    srcs = lax.axis_size("x") * lax.axis_size("y")
    scale = 2.0 / math.sqrt(width)
    chip = lax.axis_index(("x", "y"))
    core = lax.axis_index("c")
    z = lax.axis_index("z")
    slab_index = chip * 2 + core

    other = lax.ppermute(queue, "c", [(0, 1), (1, 0)])

    hi = (positions // 256).astype(BF)
    lo = (positions % 256).astype(BF)
    line = jnp.concatenate([hi, lo, jnp.zeros((width - 2 * nq,), BF)])[None]
    message = jnp.concatenate([queries, new_keys, line, jnp.zeros((ROWS - nq - nk - 1, width), BF)], axis=0)
    got = lax.all_to_all(jnp.broadcast_to(message[None], (srcs, ROWS, width)), ("x", "y"), 0, 0)

    first = jnp.stack([slab_index * slab, (slab_index ^ 1) * slab]).astype(jnp.int32)
    n = srcs * nq
    flops = 2 * n * 2 * slab * width
    out = pl.pallas_call(
        lambda *refs: partial_kernel(scale, srcs, nq, *refs),
        out_shape=jax.ShapeDtypeStruct((srcs, nq, 2 * width + 128), BF),
        in_specs=[SMEM, VMEM, VMEM, VMEM],
        out_specs=VMEM,
        scratch_shapes=[pltpu.VMEM((n, width), BF), pltpu.VMEM((n, 2 * slab), F32)],
        compiler_params=pltpu.CompilerParams(vmem_limit_bytes=40 * 1024 * 1024),
        cost_estimate=pl.CostEstimate(flops=3 * flops, bytes_accessed=4 * slab * width, transcendentals=2 * n * slab),
    )(first, got, queue, other)
    back = lax.all_to_all(out, ("x", "y"), 0, 0)

    loss, grad = pl.pallas_call(
        lambda *refs: combine_kernel(scale, srcs, nq, *refs),
        out_shape=(jax.ShapeDtypeStruct((1, 128), F32), jax.ShapeDtypeStruct((nq, width), BF)),
        in_specs=[VMEM, VMEM],
        out_specs=(VMEM, VMEM),
    )(back, queries)
    losses = loss[0, :nq]

    ring = got[:, nq:nq + nk, :][None]
    gap = nz // 2
    while gap:
        pairs = [(i, (i + gap) % nz) for i in range(nz)] + [(nz + i, nz + (i - gap) % nz) for i in range(nz)]
        came = lax.ppermute(ring, ("c", "z"), pairs)
        ring = jnp.stack([ring, came], axis=1).reshape((2 * ring.shape[0],) + ring.shape[1:])
        gap //= 2
    twin = lax.ppermute(ring, "c", [(0, 1), (1, 0)])
    low = jnp.where(core == 0, ring, twin)
    high = jnp.where(core == 0, twin, ring)
    low = jnp.roll(low[::-1], z + 1, axis=0)
    high = jnp.roll(high, z, axis=0)
    arrived = jnp.stack([low, high], axis=0).transpose(2, 0, 1, 3, 4).reshape(slab, width)
    owner = step[0] % (srcs * 2)
    updated = jnp.where(owner == slab_index, arrived, queue)
    return losses, grad, updated


def solution(mesh):
    gx, gy = mesh.devices.shape
    side = math.isqrt(gx // 2)
    fine = Mesh(np.asarray(mesh.devices).reshape(side, side, 2, gy), ("x", "y", "c", "z"))
    every = ("x", "y", "c", "z")
    return jax.shard_map(
        local,
        mesh=fine,
        in_specs=(P(every, None), P(every), P(("x", "y", "c"), None), P(every, None), P()),
        out_specs=(P(every), P(every, None), P(("x", "y", "c"), None)),
        check_vma=False,
    )
```

```python
import math

import jax
import jax.numpy as jnp
import numpy as np
from jax import lax
from jax.experimental import pallas as pl
from jax.experimental.pallas import tpu as pltpu
from jax.sharding import Mesh, PartitionSpec as P

BF = jnp.bfloat16
F32 = jnp.float32
ROWS = 48
MIB = 1024 * 1024
LOG2E = 1.4426950408889634
VMEM = pl.BlockSpec(memory_space=pltpu.VMEM)
SMEM = pl.BlockSpec(memory_space=pltpu.SMEM)


def rows_dot(a, b):
    return lax.dot_general(a, b, (((1,), (1,)), ((), ())), preferred_element_type=F32)


def partial_kernel(scale, srcs, nq, first_ref, msg_ref, own_ref, other_ref, out_ref, q_ref, s_ref):
    width = own_ref.shape[1]
    slab = own_ref.shape[0]
    n = srcs * nq
    block = 512
    lane = lax.broadcasted_iota(jnp.int32, (nq, width), 1)
    row = lax.broadcasted_iota(jnp.int32, (nq, width), 0)
    parts = []
    for j in range(srcs):
        q_ref[j * nq:(j + 1) * nq, :] = msg_ref[j, :nq, :]
        tail = msg_ref[j, nq:, :].astype(F32)
        line = tail[4:5, :] * 256.0 + tail[5:6, :]
        parts.append(jnp.sum(jnp.where(lane == row, line, 0.0), axis=1, keepdims=True))
    target = jnp.concatenate(parts, axis=0).astype(jnp.int32)
    queries = q_ref[...]
    top = None
    blocks = []
    for half, ref in enumerate((own_ref, other_ref)):
        for b in range(slab // block):
            blocks.append((half, ref, b))
    for i, (half, ref, b) in enumerate(blocks):
        s = rows_dot(queries, ref[b * block:(b + 1) * block, :])
        s_ref[:, i * block:(i + 1) * block] = s
        for c in range(block // 128):
            piece = s[:, c * 128:(c + 1) * 128]
            top = piece if top is None else jnp.maximum(top, piece)
    point = jnp.max(top, axis=1, keepdims=True).astype(BF).astype(F32)
    total = jnp.zeros((n, 128), F32)
    grad = jnp.zeros((n, width), F32)
    positive = jnp.zeros((n, width), F32)
    column = lax.broadcasted_iota(jnp.int32, (n, block), 1)
    for i, (half, ref, b) in enumerate(blocks):
        s = s_ref[:, i * block:(i + 1) * block]
        hit = column == (target - (first_ref[half] + b * block))
        e = jnp.where(hit, 0.0, jnp.exp2((s - point) * (scale * LOG2E)))
        for c in range(block // 128):
            total += e[:, c * 128:(c + 1) * 128]
        keys = ref[b * block:(b + 1) * block, :]
        grad += jnp.dot(e.astype(BF), keys, preferred_element_type=F32)
        positive += jnp.dot(hit.astype(F32).astype(BF), keys, preferred_element_type=F32)
    total = jnp.sum(total, axis=1, keepdims=True)
    t0 = total.astype(BF).astype(F32)
    t1 = (total - t0).astype(BF).astype(F32)
    t2 = total - t0 - t1
    place = lax.broadcasted_iota(jnp.int32, (n, 128), 1)
    stats = jnp.where(place == 0, point, jnp.where(place == 1, t0, jnp.where(place == 2, t1, jnp.where(place == 3, t2, 0.0))))
    stats = stats.astype(BF)
    grad = grad.astype(BF)
    positive = positive.astype(BF)
    for j in range(srcs):
        at = slice(j * nq, (j + 1) * nq)
        out_ref[j, :nq, :] = grad[at]
        out_ref[j, nq:2 * nq, :] = positive[at]
        half = nq // 2
        out_ref[j, 2 * nq:2 * nq + half, :128] = stats[j * nq:j * nq + half]
        out_ref[j, 2 * nq:2 * nq + half, 128:] = stats[j * nq + half:(j + 1) * nq]


def combine_kernel(scale, srcs, nq, got_ref, q_ref, loss_ref, grad_ref):
    width = q_ref.shape[1]
    positive = jnp.zeros((nq, width), F32)
    points, totals = [], []
    for j in range(srcs):
        positive += got_ref[j, nq:2 * nq, :].astype(F32)
        st = got_ref[j, 2 * nq:2 * nq + nq // 2, :].astype(F32)
        st = jnp.concatenate([st[:, :128], st[:, 128:]], axis=0)
        points.append(st[:, 0:1])
        totals.append(st[:, 1:2] + st[:, 2:3] + st[:, 3:4])
    s_pos = jnp.sum(q_ref[...].astype(F32) * positive, axis=1, keepdims=True)
    top = s_pos
    for p in points:
        top = jnp.maximum(top, p)
    total = jnp.exp2((s_pos - top) * (scale * LOG2E))
    grad = jnp.zeros((nq, width), F32)
    for j in range(srcs):
        a = jnp.exp2((points[j] - top) * (scale * LOG2E))
        total += a * totals[j]
        grad += a * got_ref[j, :nq, :].astype(F32)
    log_total = jnp.log(total)
    lse = top * scale + log_total
    weight = (jnp.exp(s_pos * scale - lse) - 1.0).astype(BF).astype(F32)
    grad_ref[...] = ((grad / total + weight * positive) * scale).astype(BF)
    loss = lse - s_pos * scale
    lane = lax.broadcasted_iota(jnp.int32, (nq, 128), 1)
    row = lax.broadcasted_iota(jnp.int32, (nq, 128), 0)
    loss_ref[...] = jnp.sum(jnp.where(lane == row, loss, 0.0), axis=0, keepdims=True)


def message_kernel(copies, q_ref, pos_ref, tail_ref, out_ref):
    nq = q_ref.shape[0]
    tail = tail_ref[...].astype(F32)
    row = lax.broadcasted_iota(jnp.int32, tail.shape, 0)
    high = (pos_ref[...] >> 8).astype(F32)
    low = (pos_ref[...] & 255).astype(F32)
    tail = jnp.where(row == 4, high, jnp.where(row == 5, low, tail)).astype(BF)
    for j in range(copies):
        out_ref[j, :nq, :] = q_ref[...]
        out_ref[j, nq:, :] = tail


def fill_kernel(copies, at, keys_ref, in_ref, out_ref):
    del in_ref
    keys = keys_ref[...]
    for j in range(copies):
        out_ref[j, at:at + keys.shape[0], :] = keys


def place_kernel(at, place_ref, mine_ref, twin_ref, queue_ref, out_ref):
    owner, core, z = place_ref[0], place_ref[1], place_ref[2]
    cols, rows = twin_ref.shape[0], twin_ref.shape[1]
    width = queue_ref.shape[1]

    @pl.when(owner == 0)
    def _():
        out_ref[...] = queue_ref[...]

    def put(ref, base, c):
        row = lax.broadcasted_iota(jnp.int32, (8, width), 0)
        for a in range(rows // 16):
            for b in range(4):
                tiles = []
                for k in range(4):
                    plane = 4 * b + k
                    slot = ((z - plane) if c == 0 else (plane - z)) & (cols - 1)
                    block = ref[slot, base + 16 * a:base + 16 * a + 16, :].astype(F32)
                    tiles.append((block[:8], block[8:]))
                for v in range(4):
                    t = [tiles[k][v // 2] for k in range(4)]
                    if v % 2 == 0:
                        up = jnp.where(row < 4, t[0], pltpu.roll(t[1], 4, 0))
                        down = jnp.where(row < 4, t[2], pltpu.roll(t[3], 4, 0))
                    else:
                        up = jnp.where(row < 4, pltpu.roll(t[0], 4, 0), t[1])
                        down = jnp.where(row < 4, pltpu.roll(t[2], 4, 0), t[3])
                    chip = 4 * a + v
                    start = (chip * 2 + c) * 64 + 16 * b
                    out_ref[start:start + 16, :] = jnp.concatenate([up, down], axis=0).astype(BF)

    for mine in (0, 1):
        @pl.when((owner == 1) & (core == mine))
        def _():
            put(mine_ref, at, mine)
            put(twin_ref, 0, 1 - mine)


def local(queries, positions, queue, new_keys, step):
    nq, width = queries.shape
    slab = queue.shape[0]
    nk = new_keys.shape[0]
    nz = lax.axis_size("z")
    srcs = lax.axis_size("x") * lax.axis_size("y")
    scale = 2.0 / math.sqrt(width)
    chip = lax.axis_index(("x", "y"))
    core = lax.axis_index("c")
    z = lax.axis_index("z")
    slab_index = chip * 2 + core
    swap = [(0, 1), (1, 0)]

    other = lax.ppermute(queue, "c", swap)

    message = pl.pallas_call(
        lambda *refs: message_kernel(srcs, *refs),
        out_shape=jax.ShapeDtypeStruct((srcs, ROWS, width), BF),
        in_specs=[VMEM] * 3,
        out_specs=VMEM,
        compiler_params=pltpu.CompilerParams(vmem_limit_bytes=4 * MIB),
    )(queries, jnp.pad(positions, (0, width - nq))[None], jnp.pad(new_keys, ((0, ROWS - nq - nk), (0, 0))))
    got = lax.all_to_all(message, ("x", "y"), 0, 0)

    pairs = []
    for s in range(srcs):
        for c in range(2):
            for k in range(nz):
                to = (k + s) % nz if c == 0 else (k - s) % nz
                pairs.append(((s * 2 + c) * nz + k, (s * 2 + c) * nz + to))
    plane_keys = got[:, nq:nq + nk, :].reshape(srcs * nk, width)
    moved = lax.ppermute(plane_keys, ("x", "y", "c", "z"), pairs)

    first = jnp.stack([slab_index * slab, (slab_index ^ 1) * slab]).astype(jnp.int32)
    n = srcs * nq
    at = 2 * nq + nq // 2
    flops = 2 * n * 2 * slab * width
    out_shape = jax.ShapeDtypeStruct((srcs, at + srcs * nk, width), BF)
    out = pl.pallas_call(
        lambda *refs: partial_kernel(scale, srcs, nq, *refs),
        out_shape=out_shape,
        in_specs=[SMEM, VMEM, VMEM, VMEM],
        out_specs=VMEM,
        scratch_shapes=[pltpu.VMEM((n, width), BF), pltpu.VMEM((n, 2 * slab), F32)],
        compiler_params=pltpu.CompilerParams(vmem_limit_bytes=24 * MIB),
        cost_estimate=pl.CostEstimate(flops=3 * flops, bytes_accessed=4 * slab * width, transcendentals=2 * n * slab),
    )(first, got, queue, other)
    out = pl.pallas_call(
        lambda *refs: fill_kernel(srcs, at, *refs),
        out_shape=out_shape,
        in_specs=[VMEM, VMEM],
        out_specs=VMEM,
        input_output_aliases={1: 0},
        compiler_params=pltpu.CompilerParams(vmem_limit_bytes=8 * MIB),
    )(moved, out)
    back = lax.all_to_all(out, ("x", "y"), 0, 0)

    twin = lax.ppermute(back[:, at:, :], "c", swap)
    loss, grad = pl.pallas_call(
        lambda *refs: combine_kernel(scale, srcs, nq, *refs),
        out_shape=(jax.ShapeDtypeStruct((1, 128), F32), jax.ShapeDtypeStruct((nq, width), BF)),
        in_specs=[VMEM, VMEM],
        out_specs=(VMEM, VMEM),
        compiler_params=pltpu.CompilerParams(vmem_limit_bytes=8 * MIB),
    )(back, queries)
    losses = loss[0, :nq]

    owner = (step[0] % (srcs * 2)) == slab_index
    place = jnp.stack([owner.astype(jnp.int32), core, z]).astype(jnp.int32)
    updated = pl.pallas_call(
        lambda *refs: place_kernel(at, *refs),
        out_shape=jax.ShapeDtypeStruct(queue.shape, BF),
        in_specs=[SMEM, VMEM, VMEM, VMEM],
        out_specs=VMEM,
        compiler_params=pltpu.CompilerParams(vmem_limit_bytes=12 * MIB),
    )(place, back, twin, queue)
    return losses, grad, updated


def solution(mesh):
    gx, gy = mesh.devices.shape
    side = math.isqrt(gx // 2)
    fine = Mesh(np.asarray(mesh.devices).reshape(side, side, 2, gy), ("x", "y", "c", "z"))
    every = ("x", "y", "c", "z")
    return jax.shard_map(
        local,
        mesh=fine,
        in_specs=(P(every, None), P(every), P(("x", "y", "c"), None), P(every, None), P()),
        out_specs=(P(every), P(every, None), P(("x", "y", "c"), None)),
        check_vma=False,
    )
```

```python
import math

import jax
import jax.numpy as jnp
import numpy as np
from jax import lax
from jax.experimental import pallas as pl
from jax.experimental.pallas import tpu as pltpu
from jax.sharding import Mesh, PartitionSpec as P

BF = jnp.bfloat16
F32 = jnp.float32
ROWS = 48
PIECES = 4
MIB = 1024 * 1024
LOG2E = 1.4426950408889634
VMEM = pl.BlockSpec(memory_space=pltpu.VMEM)
ANY = pl.BlockSpec(memory_space=pl.ANY)
LATE = pl.CostEstimate(flops=6 * 10**9, bytes_accessed=0, transcendentals=0)
SMEM = pl.BlockSpec(memory_space=pltpu.SMEM)


def rows_dot(a, b):
    return lax.dot_general(a, b, (((1,), (1,)), ((), ())), preferred_element_type=F32)


def partial_kernel(scale, srcs, nq, first_ref, msg_ref, own_ref, *refs):
    *other_refs, _, out_ref, q_ref, s_ref = refs
    width = own_ref.shape[1]
    slab = own_ref.shape[0]
    n = srcs * nq
    block = 512
    lane = lax.broadcasted_iota(jnp.int32, (nq, width), 1)
    row = lax.broadcasted_iota(jnp.int32, (nq, width), 0)
    parts = []
    for j in range(srcs):
        q_ref[j * nq:(j + 1) * nq, :] = msg_ref[j, :nq, :]
        tail = msg_ref[j, nq:, :].astype(F32)
        line = tail[4:5, :] * 256.0 + tail[5:6, :]
        parts.append(jnp.sum(jnp.where(lane == row, line, 0.0), axis=1, keepdims=True))
    target = jnp.concatenate(parts, axis=0).astype(jnp.int32)
    queries = q_ref[...]
    top = None
    blocks = []
    for b in range(slab // block):
        blocks.append((first_ref[0] + b * block, own_ref, b))
    cut = slab // len(other_refs)
    for i, ref in enumerate(other_refs):
        for b in range(cut // block):
            blocks.append((first_ref[1] + i * cut + b * block, ref, b))
    for i, (start, ref, b) in enumerate(blocks):
        s = rows_dot(queries, ref[b * block:(b + 1) * block, :])
        s_ref[:, i * block:(i + 1) * block] = s
        for c in range(block // 128):
            piece = s[:, c * 128:(c + 1) * 128]
            top = piece if top is None else jnp.maximum(top, piece)
    point = jnp.max(top, axis=1, keepdims=True).astype(BF).astype(F32)
    total = jnp.zeros((n, 128), F32)
    grad = jnp.zeros((n, width), F32)
    positive = jnp.zeros((n, width), F32)
    column = lax.broadcasted_iota(jnp.int32, (n, block), 1)
    for i, (start, ref, b) in enumerate(blocks):
        s = s_ref[:, i * block:(i + 1) * block]
        hit = column == (target - start)
        e = jnp.where(hit, 0.0, jnp.exp2((s - point) * (scale * LOG2E)))
        for c in range(block // 128):
            total += e[:, c * 128:(c + 1) * 128]
        keys = ref[b * block:(b + 1) * block, :]
        grad += jnp.dot(e.astype(BF), keys, preferred_element_type=F32)
        positive += jnp.dot(hit.astype(F32).astype(BF), keys, preferred_element_type=F32)
    total = jnp.sum(total, axis=1, keepdims=True)
    t0 = total.astype(BF).astype(F32)
    t1 = (total - t0).astype(BF).astype(F32)
    t2 = total - t0 - t1
    place = lax.broadcasted_iota(jnp.int32, (n, 128), 1)
    stats = jnp.where(place == 0, point, jnp.where(place == 1, t0, jnp.where(place == 2, t1, jnp.where(place == 3, t2, 0.0))))
    stats = stats.astype(BF)
    grad = grad.astype(BF)
    positive = positive.astype(BF)
    for j in range(srcs):
        at = slice(j * nq, (j + 1) * nq)
        out_ref[j, :nq, :] = grad[at]
        out_ref[j, nq:2 * nq, :] = positive[at]
        half = nq // 2
        out_ref[j, 2 * nq:2 * nq + half, :128] = stats[j * nq:j * nq + half]
        out_ref[j, 2 * nq:2 * nq + half, 128:] = stats[j * nq + half:(j + 1) * nq]


def combine_kernel(scale, srcs, nq, got_ref, q_ref, loss_ref, grad_ref):
    width = q_ref.shape[1]
    positive = jnp.zeros((nq, width), F32)
    points, totals = [], []
    for j in range(srcs):
        positive += got_ref[j, nq:2 * nq, :].astype(F32)
        st = got_ref[j, 2 * nq:2 * nq + nq // 2, :].astype(F32)
        st = jnp.concatenate([st[:, :128], st[:, 128:]], axis=0)
        points.append(st[:, 0:1])
        totals.append(st[:, 1:2] + st[:, 2:3] + st[:, 3:4])
    s_pos = jnp.sum(q_ref[...].astype(F32) * positive, axis=1, keepdims=True)
    top = s_pos
    for p in points:
        top = jnp.maximum(top, p)
    total = jnp.exp2((s_pos - top) * (scale * LOG2E))
    grad = jnp.zeros((nq, width), F32)
    for j in range(srcs):
        a = jnp.exp2((points[j] - top) * (scale * LOG2E))
        total += a * totals[j]
        grad += a * got_ref[j, :nq, :].astype(F32)
    log_total = jnp.log(total)
    lse = top * scale + log_total
    weight = (jnp.exp(s_pos * scale - lse) - 1.0).astype(BF).astype(F32)
    grad_ref[...] = ((grad / total + weight * positive) * scale).astype(BF)
    loss = lse - s_pos * scale
    lane = lax.broadcasted_iota(jnp.int32, (nq, 128), 1)
    row = lax.broadcasted_iota(jnp.int32, (nq, 128), 0)
    loss_ref[...] = jnp.sum(jnp.where(lane == row, loss, 0.0), axis=0, keepdims=True)


def message_kernel(copies, q_ref, pos_ref, keys_ref, out_ref, tail_ref):
    nq, nk = q_ref.shape[0], keys_ref.shape[0]
    tail_ref[...] = jnp.zeros_like(tail_ref)
    tail_ref[:nk, :] = keys_ref[...].astype(F32)
    tail_ref[nk:nk + 1, :nq] = (pos_ref[...] >> 8).astype(F32)
    tail_ref[nk + 1:nk + 2, :nq] = (pos_ref[...] & 255).astype(F32)
    tail = tail_ref[...].astype(BF)
    for j in range(copies):
        out_ref[j, :nq, :] = q_ref[...]
        out_ref[j, nq:, :] = tail


def copies_kernel(copies, keys_ref, after_ref, out_ref):
    del after_ref
    for j in range(copies):
        out_ref[j] = keys_ref[...]


def gate_kernel(after_ref, out_ref):
    del after_ref
    out_ref[...] = jnp.zeros_like(out_ref)


def plane_keys_kernel(nq, got_ref, after_ref, out_ref):
    del after_ref
    width = out_ref.shape[1]
    row = lax.broadcasted_iota(jnp.int32, (8, width), 0)
    for a in range(got_ref.shape[0] // 4):
        t = [got_ref[4 * a + k, nq:, :].astype(F32)[:8] for k in range(4)]
        up = jnp.where(row < 4, t[0], pltpu.roll(t[1], 4, 0))
        down = jnp.where(row < 4, t[2], pltpu.roll(t[3], 4, 0))
        out_ref[16 * a:16 * a + 16, :] = jnp.concatenate([up, down], axis=0).astype(BF)


def place_kernel(place_ref, mine_ref, twin_ref, queue_ref, out_ref):
    owner, core, z = place_ref[0], place_ref[1], place_ref[2]
    cols, rows = twin_ref.shape[0], twin_ref.shape[1]
    width = queue_ref.shape[1]

    @pl.when(owner == 0)
    def _():
        out_ref[...] = queue_ref[...]

    def put(ref, c):
        row = lax.broadcasted_iota(jnp.int32, (8, width), 0)
        for a in range(rows // 16):
            for b in range(4):
                tiles = []
                for k in range(4):
                    plane = 4 * b + k
                    slot = ((z - plane) if c == 0 else (plane - z)) & (cols - 1)
                    block = ref[slot, 16 * a:16 * a + 16, :].astype(F32)
                    tiles.append((block[:8], block[8:]))
                for v in range(4):
                    t = [tiles[k][v // 2] for k in range(4)]
                    if v % 2 == 0:
                        up = jnp.where(row < 4, t[0], pltpu.roll(t[1], 4, 0))
                        down = jnp.where(row < 4, t[2], pltpu.roll(t[3], 4, 0))
                    else:
                        up = jnp.where(row < 4, pltpu.roll(t[0], 4, 0), t[1])
                        down = jnp.where(row < 4, pltpu.roll(t[2], 4, 0), t[3])
                    chip = 4 * a + v
                    start = (chip * 2 + c) * 64 + 16 * b
                    out_ref[start:start + 16, :] = jnp.concatenate([up, down], axis=0).astype(BF)

    for mine in (0, 1):
        @pl.when((owner == 1) & (core == mine))
        def _():
            put(mine_ref, mine)
            put(twin_ref, 1 - mine)


def local(queries, positions, queue, new_keys, step):
    nq, width = queries.shape
    slab = queue.shape[0]
    nk = new_keys.shape[0]
    nz = lax.axis_size("z")
    srcs = lax.axis_size("x") * lax.axis_size("y")
    scale = 2.0 / math.sqrt(width)
    chip = lax.axis_index(("x", "y"))
    core = lax.axis_index("c")
    z = lax.axis_index("z")
    slab_index = chip * 2 + core
    swap = [(0, 1), (1, 0)]

    message = pl.pallas_call(
        lambda *refs: message_kernel(srcs, *refs),
        out_shape=jax.ShapeDtypeStruct((srcs, ROWS, width), BF),
        in_specs=[VMEM] * 3,
        out_specs=VMEM,
        scratch_shapes=[pltpu.VMEM((ROWS - nq, width), F32)],
        compiler_params=pltpu.CompilerParams(vmem_limit_bytes=56 * MIB),
    )(queries, positions[None], new_keys)
    got = lax.all_to_all(message, ("x", "y"), 0, 0)
    gate = pl.pallas_call(
        gate_kernel,
        out_shape=jax.ShapeDtypeStruct((8, 128), F32),
        in_specs=[ANY],
        out_specs=VMEM,
        compiler_params=pltpu.CompilerParams(vmem_limit_bytes=MIB),
        cost_estimate=LATE,
    )(message)
    slab_keys, gate = lax.optimization_barrier((queue, gate))
    cut = slab // PIECES
    other = [lax.ppermute(slab_keys[i * cut:(i + 1) * cut], "c", swap) for i in range(PIECES)]

    first = jnp.stack([slab_index * slab, (slab_index ^ 1) * slab]).astype(jnp.int32)
    n = srcs * nq
    flops = 2 * n * 2 * slab * width
    out = pl.pallas_call(
        lambda *refs: partial_kernel(scale, srcs, nq, *refs),
        out_shape=jax.ShapeDtypeStruct((srcs, 2 * nq + nq // 2, width), BF),
        in_specs=[SMEM, VMEM, VMEM] + [VMEM] * PIECES + [ANY],
        out_specs=VMEM,
        scratch_shapes=[pltpu.VMEM((n, width), BF), pltpu.VMEM((n, 2 * slab), F32)],
        compiler_params=pltpu.CompilerParams(vmem_limit_bytes=24 * MIB),
        cost_estimate=pl.CostEstimate(flops=3 * flops, bytes_accessed=4 * slab * width, transcendentals=2 * n * slab),
    )(first, got, queue, *other, gate)
    back = lax.all_to_all(out, ("x", "y"), 0, 0)
    plane_keys = pl.pallas_call(
        lambda *refs: plane_keys_kernel(nq, *refs),
        out_shape=jax.ShapeDtypeStruct((srcs * nk, width), BF),
        in_specs=[VMEM, ANY],
        out_specs=VMEM,
        compiler_params=pltpu.CompilerParams(vmem_limit_bytes=4 * MIB),
        cost_estimate=LATE,
    )(got, out)

    pairs = []
    for s in range(srcs):
        for c in range(2):
            for k in range(nz):
                to = (k + s) % nz if c == 0 else (k - s) % nz
                pairs.append(((s * 2 + c) * nz + k, (s * 2 + c) * nz + to))
    moved = lax.ppermute(plane_keys, ("x", "y", "c", "z"), pairs)
    mine = lax.all_to_all(
        pl.pallas_call(
            lambda *refs: copies_kernel(srcs, *refs),
            out_shape=jax.ShapeDtypeStruct((srcs, srcs * nk, width), BF),
            in_specs=[VMEM, ANY],
            out_specs=VMEM,
            compiler_params=pltpu.CompilerParams(vmem_limit_bytes=4 * MIB),
        )(moved, back),
        ("x", "y"), 0, 0,
    )
    twin = lax.ppermute(mine, "c", swap)

    loss, grad = pl.pallas_call(
        lambda *refs: combine_kernel(scale, srcs, nq, *refs),
        out_shape=(jax.ShapeDtypeStruct((1, 128), F32), jax.ShapeDtypeStruct((nq, width), BF)),
        in_specs=[VMEM, VMEM],
        out_specs=(VMEM, VMEM),
        compiler_params=pltpu.CompilerParams(vmem_limit_bytes=8 * MIB),
    )(back, queries)
    losses = loss[0, :nq]

    owner = (step[0] % (srcs * 2)) == slab_index
    place = jnp.stack([owner.astype(jnp.int32), core, z]).astype(jnp.int32)
    updated = pl.pallas_call(
        place_kernel,
        out_shape=jax.ShapeDtypeStruct(queue.shape, BF),
        in_specs=[SMEM, VMEM, VMEM, VMEM],
        out_specs=VMEM,
        compiler_params=pltpu.CompilerParams(vmem_limit_bytes=12 * MIB),
    )(place, mine, twin, queue)
    return losses, grad, updated


def solution(mesh):
    gx, gy = mesh.devices.shape
    side = math.isqrt(gx // 2)
    fine = Mesh(np.asarray(mesh.devices).reshape(side, side, 2, gy), ("x", "y", "c", "z"))
    every = ("x", "y", "c", "z")
    return jax.shard_map(
        local,
        mesh=fine,
        in_specs=(P(every, None), P(every), P(("x", "y", "c"), None), P(every, None), P()),
        out_specs=(P(every), P(every, None), P(("x", "y", "c"), None)),
        check_vma=False,
    )
```

```python
import math

import jax
import jax.numpy as jnp
import numpy as np
from jax import lax
from jax.experimental import pallas as pl
from jax.experimental.pallas import tpu as pltpu
from jax.sharding import Mesh, PartitionSpec as P

BF = jnp.bfloat16
F32 = jnp.float32
ROWS = 48
MIB = 1024 * 1024
LOG2E = 1.4426950408889634
VMEM = pl.BlockSpec(memory_space=pltpu.VMEM)
ANY = pl.BlockSpec(memory_space=pl.ANY)
LATE = pl.CostEstimate(flops=6 * 10**9, bytes_accessed=0, transcendentals=0)
EARLY = pl.CostEstimate(flops=92 * 10**8, bytes_accessed=0, transcendentals=0)
SMEM = pl.BlockSpec(memory_space=pltpu.SMEM)


def rows_dot(a, b):
    return lax.dot_general(a, b, (((1,), (1,)), ((), ())), preferred_element_type=F32)


def partial_kernel(scale, srcs, nq, first_ref, msg_ref, own_ref, *refs):
    other_ref, _, _, out_ref, q_ref, s_ref = refs
    width = own_ref.shape[1]
    slab = own_ref.shape[0]
    n = srcs * nq
    block = 256
    lane = lax.broadcasted_iota(jnp.int32, (nq, width), 1)
    row = lax.broadcasted_iota(jnp.int32, (nq, width), 0)
    parts = []
    for j in range(srcs):
        q_ref[j * nq:(j + 1) * nq, :] = msg_ref[j, :nq, :]
        tail = msg_ref[j, nq:, :].astype(F32)
        line = tail[4:5, :] * 256.0 + tail[5:6, :]
        parts.append(jnp.sum(jnp.where(lane == row, line, 0.0), axis=1, keepdims=True))
    target = jnp.concatenate(parts, axis=0).astype(jnp.int32)
    queries = q_ref[...]
    top = None
    blocks = []
    for b in range(slab // block):
        blocks.append((first_ref[0] + b * block, own_ref, b))
    for b in range(slab // block):
        blocks.append((first_ref[1] + b * block, other_ref, b))
    for i, (start, ref, b) in enumerate(blocks):
        s = rows_dot(queries, ref[b * block:(b + 1) * block, :])
        s_ref[:, i * block:(i + 1) * block] = s
        for c in range(block // 128):
            piece = s[:, c * 128:(c + 1) * 128]
            top = piece if top is None else jnp.maximum(top, piece)
    point = jnp.max(top, axis=1, keepdims=True).astype(BF).astype(F32)
    total = jnp.zeros((n, 128), F32)
    grad = jnp.zeros((n, width), F32)
    positive = jnp.zeros((n, width), F32)
    column = lax.broadcasted_iota(jnp.int32, (n, block), 1)
    for i, (start, ref, b) in enumerate(blocks):
        s = s_ref[:, i * block:(i + 1) * block]
        hit = column == (target - start)
        e = jnp.where(hit, 0.0, jnp.exp2((s - point) * (scale * LOG2E)))
        for c in range(block // 128):
            total += e[:, c * 128:(c + 1) * 128]
        keys = ref[b * block:(b + 1) * block, :]
        grad += jnp.dot(e.astype(BF), keys, preferred_element_type=F32)
        positive += jnp.dot(hit.astype(F32).astype(BF), keys, preferred_element_type=F32)
    total = jnp.sum(total, axis=1, keepdims=True)
    t0 = total.astype(BF).astype(F32)
    t1 = (total - t0).astype(BF).astype(F32)
    t2 = total - t0 - t1
    place = lax.broadcasted_iota(jnp.int32, (n, 128), 1)
    stats = jnp.where(place == 0, point, jnp.where(place == 1, t0, jnp.where(place == 2, t1, jnp.where(place == 3, t2, 0.0))))
    stats = stats.astype(BF)
    grad = grad.astype(BF)
    positive = positive.astype(BF)
    for j in range(srcs):
        at = slice(j * nq, (j + 1) * nq)
        out_ref[j, :nq, :] = grad[at]
        out_ref[j, nq:2 * nq, :] = positive[at]
        half = nq // 2
        out_ref[j, 2 * nq:2 * nq + half, :128] = stats[j * nq:j * nq + half]
        out_ref[j, 2 * nq:2 * nq + half, 128:] = stats[j * nq + half:(j + 1) * nq]


def combine_kernel(scale, srcs, nq, got_ref, q_ref, loss_ref, grad_ref):
    width = q_ref.shape[1]
    positive = jnp.zeros((nq, width), F32)
    points, totals = [], []
    for j in range(srcs):
        positive += got_ref[j, nq:2 * nq, :].astype(F32)
        st = got_ref[j, 2 * nq:2 * nq + nq // 2, :].astype(F32)
        st = jnp.concatenate([st[:, :128], st[:, 128:]], axis=0)
        points.append(st[:, 0:1])
        totals.append(st[:, 1:2] + st[:, 2:3] + st[:, 3:4])
    s_pos = jnp.sum(q_ref[...].astype(F32) * positive, axis=1, keepdims=True)
    top = s_pos
    for p in points:
        top = jnp.maximum(top, p)
    total = jnp.exp2((s_pos - top) * (scale * LOG2E))
    grad = jnp.zeros((nq, width), F32)
    for j in range(srcs):
        a = jnp.exp2((points[j] - top) * (scale * LOG2E))
        total += a * totals[j]
        grad += a * got_ref[j, :nq, :].astype(F32)
    log_total = jnp.log(total)
    lse = top * scale + log_total
    weight = (jnp.exp(s_pos * scale - lse) - 1.0).astype(BF).astype(F32)
    grad_ref[...] = ((grad / total + weight * positive) * scale).astype(BF)
    loss = lse - s_pos * scale
    lane = lax.broadcasted_iota(jnp.int32, (nq, 128), 1)
    row = lax.broadcasted_iota(jnp.int32, (nq, 128), 0)
    loss_ref[...] = jnp.sum(jnp.where(lane == row, loss, 0.0), axis=0, keepdims=True)


def message_kernel(copies, q_ref, pos_ref, keys_ref, out_ref, tail_ref):
    nq, nk = q_ref.shape[0], keys_ref.shape[0]
    tail_ref[...] = jnp.zeros_like(tail_ref)
    tail_ref[:nk, :] = keys_ref[...].astype(F32)
    tail_ref[nk:nk + 1, :nq] = (pos_ref[...] >> 8).astype(F32)
    tail_ref[nk + 1:nk + 2, :nq] = (pos_ref[...] & 255).astype(F32)
    tail = tail_ref[...].astype(BF)
    for j in range(copies):
        out_ref[j, :nq, :] = q_ref[...]
        out_ref[j, nq:, :] = tail


def fill_kernel(copies, at, keys_ref, in_ref, out_ref):
    del in_ref
    keys = keys_ref[...]
    for j in range(copies):
        out_ref[j, at:at + keys.shape[0], :] = keys


def gate_kernel(after_ref, out_ref):
    del after_ref
    out_ref[...] = jnp.zeros_like(out_ref)


def plane_keys_kernel(nq, got_ref, out_ref):
    width = out_ref.shape[1]
    row = lax.broadcasted_iota(jnp.int32, (8, width), 0)
    for a in range(got_ref.shape[0] // 4):
        t = [got_ref[4 * a + k, nq:, :].astype(F32)[:8] for k in range(4)]
        up = jnp.where(row < 4, t[0], pltpu.roll(t[1], 4, 0))
        down = jnp.where(row < 4, t[2], pltpu.roll(t[3], 4, 0))
        out_ref[16 * a:16 * a + 16, :] = jnp.concatenate([up, down], axis=0).astype(BF)


def place_kernel(at, place_ref, mine_ref, twin_ref, queue_ref, out_ref):
    owner, core, z = place_ref[0], place_ref[1], place_ref[2]
    cols, rows = twin_ref.shape[0], twin_ref.shape[1]
    width = queue_ref.shape[1]

    @pl.when(owner == 0)
    def _():
        out_ref[...] = queue_ref[...]

    def put(ref, base, c):
        row = lax.broadcasted_iota(jnp.int32, (8, width), 0)
        for a in range(rows // 16):
            for b in range(4):
                tiles = []
                for k in range(4):
                    plane = 4 * b + k
                    slot = ((z - plane) if c == 0 else (plane - z)) & (cols - 1)
                    block = ref[slot, base + 16 * a:base + 16 * a + 16, :].astype(F32)
                    tiles.append((block[:8], block[8:]))
                for v in range(4):
                    t = [tiles[k][v // 2] for k in range(4)]
                    if v % 2 == 0:
                        up = jnp.where(row < 4, t[0], pltpu.roll(t[1], 4, 0))
                        down = jnp.where(row < 4, t[2], pltpu.roll(t[3], 4, 0))
                    else:
                        up = jnp.where(row < 4, pltpu.roll(t[0], 4, 0), t[1])
                        down = jnp.where(row < 4, pltpu.roll(t[2], 4, 0), t[3])
                    chip = 4 * a + v
                    start = (chip * 2 + c) * 64 + 16 * b
                    out_ref[start:start + 16, :] = jnp.concatenate([up, down], axis=0).astype(BF)

    for mine in (0, 1):
        @pl.when((owner == 1) & (core == mine))
        def _():
            put(mine_ref, at, mine)
            put(twin_ref, 0, 1 - mine)


def local(queries, positions, queue, new_keys, step):
    nq, width = queries.shape
    slab = queue.shape[0]
    nk = new_keys.shape[0]
    nz = lax.axis_size("z")
    srcs = lax.axis_size("x") * lax.axis_size("y")
    scale = 2.0 / math.sqrt(width)
    chip = lax.axis_index(("x", "y"))
    core = lax.axis_index("c")
    z = lax.axis_index("z")
    slab_index = chip * 2 + core
    swap = [(0, 1), (1, 0)]

    message = pl.pallas_call(
        lambda *refs: message_kernel(srcs, *refs),
        out_shape=jax.ShapeDtypeStruct((srcs, ROWS, width), BF),
        in_specs=[VMEM] * 3,
        out_specs=VMEM,
        scratch_shapes=[pltpu.VMEM((ROWS - nq, width), F32)],
        compiler_params=pltpu.CompilerParams(vmem_limit_bytes=56 * MIB),
    )(queries, positions[None], new_keys)
    got = lax.all_to_all(message, ("x", "y"), 0, 0)
    gate = pl.pallas_call(
        gate_kernel,
        out_shape=jax.ShapeDtypeStruct((8, 128), F32),
        in_specs=[ANY],
        out_specs=VMEM,
        compiler_params=pltpu.CompilerParams(vmem_limit_bytes=MIB),
        cost_estimate=LATE,
    )(message)
    slab_keys, gate = lax.optimization_barrier((queue, gate))
    other = lax.ppermute(slab_keys, "c", swap)

    plane_keys = pl.pallas_call(
        lambda *refs: plane_keys_kernel(nq, *refs),
        out_shape=jax.ShapeDtypeStruct((srcs * nk, width), BF),
        in_specs=[VMEM],
        out_specs=VMEM,
        compiler_params=pltpu.CompilerParams(vmem_limit_bytes=4 * MIB),
        cost_estimate=EARLY,
    )(got)
    pairs = []
    for s in range(srcs):
        for c in range(2):
            for k in range(nz):
                to = (k + s) % nz if c == 0 else (k - s) % nz
                pairs.append(((s * 2 + c) * nz + k, (s * 2 + c) * nz + to))
    moved = lax.ppermute(plane_keys, ("x", "y", "c", "z"), pairs)

    first = jnp.stack([slab_index * slab, (slab_index ^ 1) * slab]).astype(jnp.int32)
    n = srcs * nq
    at = 2 * nq + nq // 2
    flops = 2 * n * 2 * slab * width
    out_shape = jax.ShapeDtypeStruct((srcs, at + srcs * nk, width), BF)
    out = pl.pallas_call(
        lambda *refs: partial_kernel(scale, srcs, nq, *refs),
        out_shape=out_shape,
        in_specs=[SMEM, VMEM, VMEM, VMEM, ANY, ANY],
        out_specs=VMEM,
        scratch_shapes=[pltpu.VMEM((n, width), BF), pltpu.VMEM((n, 2 * slab), F32)],
        compiler_params=pltpu.CompilerParams(vmem_limit_bytes=24 * MIB),
        cost_estimate=pl.CostEstimate(flops=3 * flops, bytes_accessed=4 * slab * width, transcendentals=2 * n * slab),
    )(first, got, queue, other, gate, plane_keys)
    out = pl.pallas_call(
        lambda *refs: fill_kernel(srcs, at, *refs),
        out_shape=out_shape,
        in_specs=[VMEM, VMEM],
        out_specs=VMEM,
        input_output_aliases={1: 0},
        compiler_params=pltpu.CompilerParams(vmem_limit_bytes=8 * MIB),
    )(moved, out)
    back = lax.all_to_all(out, ("x", "y"), 0, 0)
    twin = lax.ppermute(back[:, at:, :], "c", swap)

    loss, grad = pl.pallas_call(
        lambda *refs: combine_kernel(scale, srcs, nq, *refs),
        out_shape=(jax.ShapeDtypeStruct((1, 128), F32), jax.ShapeDtypeStruct((nq, width), BF)),
        in_specs=[VMEM, VMEM],
        out_specs=(VMEM, VMEM),
        compiler_params=pltpu.CompilerParams(vmem_limit_bytes=8 * MIB),
    )(back, queries)
    losses = loss[0, :nq]

    owner = (step[0] % (srcs * 2)) == slab_index
    place = jnp.stack([owner.astype(jnp.int32), core, z]).astype(jnp.int32)
    updated = pl.pallas_call(
        lambda *refs: place_kernel(at, *refs),
        out_shape=jax.ShapeDtypeStruct(queue.shape, BF),
        in_specs=[SMEM, VMEM, VMEM, VMEM],
        out_specs=VMEM,
        compiler_params=pltpu.CompilerParams(vmem_limit_bytes=12 * MIB),
    )(place, back, twin, queue)
    return losses, grad, updated


def solution(mesh):
    gx, gy = mesh.devices.shape
    side = math.isqrt(gx // 2)
    fine = Mesh(np.asarray(mesh.devices).reshape(side, side, 2, gy), ("x", "y", "c", "z"))
    every = ("x", "y", "c", "z")
    return jax.shard_map(
        local,
        mesh=fine,
        in_specs=(P(every, None), P(every), P(("x", "y", "c"), None), P(every, None), P()),
        out_specs=(P(every), P(every, None), P(("x", "y", "c"), None)),
        check_vma=False,
    )
```

```python
import math

import jax
import jax.numpy as jnp
import numpy as np
from jax import lax
from jax.experimental import pallas as pl
from jax.experimental.pallas import tpu as pltpu
from jax.sharding import Mesh, PartitionSpec as P

BF = jnp.bfloat16
F32 = jnp.float32
ROWS = 40
MIB = 1024 * 1024
LOG2E = 1.4426950408889634
VMEM = pl.BlockSpec(memory_space=pltpu.VMEM)
ANY = pl.BlockSpec(memory_space=pl.ANY)
LATE = pl.CostEstimate(flops=6 * 10**9, bytes_accessed=0, transcendentals=0)
EARLY = pl.CostEstimate(flops=92 * 10**8, bytes_accessed=0, transcendentals=0)
SMEM = pl.BlockSpec(memory_space=pltpu.SMEM)


def rows_dot(a, b):
    return lax.dot_general(a, b, (((1,), (1,)), ((), ())), preferred_element_type=F32)


def partial_kernel(scale, srcs, nq, info_ref, msg_ref, own_ref, *refs):
    other_ref, _, out_ref, q_ref, s_ref = refs
    width = own_ref.shape[1]
    slab = own_ref.shape[0]
    n = srcs * nq
    block = 256
    lane = lax.broadcasted_iota(jnp.int32, (nq, width), 1)
    row = lax.broadcasted_iota(jnp.int32, (nq, width), 0)
    parts = []
    for j in range(srcs):
        q_ref[j * nq:(j + 1) * nq, :] = msg_ref[j, :nq, :]
        tail = msg_ref[j, nq:, :].astype(F32)
        line = tail[4:5, :] * 256.0 + tail[5:6, :]
        parts.append(jnp.sum(jnp.where(lane == row, line, 0.0), axis=1, keepdims=True))
    target = jnp.concatenate(parts, axis=0).astype(jnp.int32)
    queries = q_ref[...]
    top = None
    blocks = []
    for b in range(slab // block):
        blocks.append((info_ref[0] + b * block, own_ref, b))
    for b in range(slab // block):
        blocks.append((info_ref[1] + b * block, other_ref, b))
    for i, (start, ref, b) in enumerate(blocks):
        s = rows_dot(queries, ref[b * block:(b + 1) * block, :])
        s_ref[:, i * block:(i + 1) * block] = s
        for c in range(block // 128):
            piece = s[:, c * 128:(c + 1) * 128]
            top = piece if top is None else jnp.maximum(top, piece)
    point = jnp.max(top, axis=1, keepdims=True).astype(BF).astype(F32)
    total = jnp.zeros((n, 128), F32)
    grad = jnp.zeros((n, width), F32)
    positive = jnp.zeros((n, width), F32)
    column = lax.broadcasted_iota(jnp.int32, (n, block), 1)
    for i, (start, ref, b) in enumerate(blocks):
        s = s_ref[:, i * block:(i + 1) * block]
        hit = column == (target - start)
        e = jnp.where(hit, 0.0, jnp.exp2((s - point) * (scale * LOG2E)))
        for c in range(block // 128):
            total += e[:, c * 128:(c + 1) * 128]
        keys = ref[b * block:(b + 1) * block, :]
        grad += jnp.dot(e.astype(BF), keys, preferred_element_type=F32)
        positive += jnp.dot(hit.astype(F32).astype(BF), keys, preferred_element_type=F32)
    total = jnp.sum(total, axis=1, keepdims=True)
    t0 = total.astype(BF).astype(F32)
    t1 = (total - t0).astype(BF).astype(F32)
    t2 = total - t0 - t1
    stats = (point, t0, t1, t2)
    grad = grad.astype(BF)
    positive = positive.astype(BF)
    for j in range(srcs):
        at = slice(j * nq, (j + 1) * nq)
        out_ref[j, :nq, :] = grad[at]
        out_ref[j, nq:2 * nq, :] = positive[at]
    lane = lax.broadcasted_iota(jnp.int32, (nq, width), 1)
    row = lax.broadcasted_iota(jnp.int32, (nq, width), 0)
    for j in range(srcs):
        at = slice(j * nq, (j + 1) * nq)
        line = jnp.zeros((nq, width), F32)
        for k, value in enumerate(stats):
            line = jnp.where(lane == row + k * nq, value[at], line)
        line = jnp.sum(line, axis=0, keepdims=True)
        out_ref[j, out_ref.shape[1] - 8:, :] = jnp.broadcast_to(line, (8, width)).astype(BF)


def combine_kernel(scale, srcs, nq, got_ref, q_ref, loss_ref, grad_ref):
    width = q_ref.shape[1]
    lane = lax.broadcasted_iota(jnp.int32, (nq, 128), 1)
    row = lax.broadcasted_iota(jnp.int32, (nq, 128), 0)
    positive = jnp.zeros((nq, width), F32)
    points, totals = [], []
    for j in range(srcs):
        positive += got_ref[j, nq:2 * nq, :].astype(F32)
        st = jnp.broadcast_to(got_ref[j, got_ref.shape[1] - 8:, :].astype(F32)[:1, :128], (nq, 128))
        points.append(jnp.sum(jnp.where(lane == row, st, 0.0), axis=1, keepdims=True))
        three = (lane >= nq) & (lane % nq == row)
        totals.append(jnp.sum(jnp.where(three, st, 0.0), axis=1, keepdims=True))
    s_pos = jnp.sum(q_ref[...].astype(F32) * positive, axis=1, keepdims=True)
    top = s_pos
    for p in points:
        top = jnp.maximum(top, p)
    total = jnp.exp2((s_pos - top) * (scale * LOG2E))
    grad = jnp.zeros((nq, width), F32)
    for j in range(srcs):
        a = jnp.exp2((points[j] - top) * (scale * LOG2E))
        total += a * totals[j]
        grad += a * got_ref[j, :nq, :].astype(F32)
    log_total = jnp.log(total)
    lse = top * scale + log_total
    weight = (jnp.exp(s_pos * scale - lse) - 1.0).astype(BF).astype(F32)
    grad_ref[...] = ((grad / total + weight * positive) * scale).astype(BF)
    loss = lse - s_pos * scale
    loss_ref[...] = jnp.sum(jnp.where(lane == row, loss, 0.0), axis=0, keepdims=True)[:, :nq]


def message_kernel(copies, q_ref, pos_ref, keys_ref, out_ref, tail_ref):
    nq, nk = q_ref.shape[0], keys_ref.shape[0]
    tail_ref[...] = jnp.zeros_like(tail_ref)
    tail_ref[:nk, :] = keys_ref[...].astype(F32)
    tail_ref[nk:nk + 1, :nq] = (pos_ref[...] >> 8).astype(F32)
    tail_ref[nk + 1:nk + 2, :nq] = (pos_ref[...] & 255).astype(F32)
    tail = tail_ref[...].astype(BF)
    for j in range(copies):
        out_ref[j, :nq, :] = q_ref[...]
        out_ref[j, nq:, :] = tail


def fill_kernel(copies, at, keys_ref, in_ref, out_ref):
    del in_ref
    keys = keys_ref[...]
    for j in range(copies):
        out_ref[j, at:at + keys.shape[0], :] = keys


def slab_kernel(after_ref, queue_ref, out_ref, sem):
    del after_ref
    copy = pltpu.make_async_copy(queue_ref, out_ref, sem)
    copy.start()
    copy.wait()


def plane_keys_kernel(nq, got_ref, out_ref):
    width = out_ref.shape[1]
    row = lax.broadcasted_iota(jnp.int32, (8, width), 0)
    for a in range(got_ref.shape[0] // 4):
        t = [got_ref[4 * a + k, nq:, :].astype(F32)[:8] for k in range(4)]
        up = jnp.where(row < 4, t[0], pltpu.roll(t[1], 4, 0))
        down = jnp.where(row < 4, t[2], pltpu.roll(t[3], 4, 0))
        out_ref[16 * a:16 * a + 16, :] = jnp.concatenate([up, down], axis=0).astype(BF)


def place_kernel(at, info_ref, mine_ref, twin_ref, queue_ref, out_ref, new_ref, sem):
    del queue_ref
    owner, core, z = info_ref[2], info_ref[3], info_ref[4]
    cols, rows = twin_ref.shape[0], twin_ref.shape[1]
    width = twin_ref.shape[2]

    def put(ref, base, c):
        row = lax.broadcasted_iota(jnp.int32, (8, width), 0)
        for a in range(rows // 16):
            for b in range(4):
                tiles = []
                for k in range(4):
                    plane = 4 * b + k
                    slot = ((z - plane) if c == 0 else (plane - z)) & (cols - 1)
                    block = ref[slot, base + 16 * a:base + 16 * a + 16, :].astype(F32)
                    tiles.append((block[:8], block[8:]))
                for v in range(4):
                    t = [tiles[k][v // 2] for k in range(4)]
                    if v % 2 == 0:
                        up = jnp.where(row < 4, t[0], pltpu.roll(t[1], 4, 0))
                        down = jnp.where(row < 4, t[2], pltpu.roll(t[3], 4, 0))
                    else:
                        up = jnp.where(row < 4, pltpu.roll(t[0], 4, 0), t[1])
                        down = jnp.where(row < 4, pltpu.roll(t[2], 4, 0), t[3])
                    chip = 4 * a + v
                    start = (chip * 2 + c) * 64 + 16 * b
                    new_ref[start:start + 16, :] = jnp.concatenate([up, down], axis=0).astype(BF)

    for mine in (0, 1):
        @pl.when((owner == 1) & (core == mine))
        def _():
            put(mine_ref, at, mine)
            put(twin_ref, 0, 1 - mine)

    @pl.when(owner == 1)
    def _():
        copy = pltpu.make_async_copy(new_ref, out_ref, sem)
        copy.start()
        copy.wait()


def local(queries, positions, queue, new_keys, step):
    nq, width = queries.shape
    slab = queue.shape[0]
    nk = new_keys.shape[0]
    nz = lax.axis_size("z")
    srcs = lax.axis_size("x") * lax.axis_size("y")
    scale = 2.0 / math.sqrt(width)
    chip = lax.axis_index(("x", "y"))
    core = lax.axis_index("c")
    z = lax.axis_index("z")
    slab_index = chip * 2 + core
    swap = [(0, 1), (1, 0)]

    message = pl.pallas_call(
        lambda *refs: message_kernel(srcs, *refs),
        out_shape=jax.ShapeDtypeStruct((srcs, ROWS, width), BF),
        in_specs=[VMEM] * 3,
        out_specs=VMEM,
        scratch_shapes=[pltpu.VMEM((ROWS - nq, width), F32)],
        compiler_params=pltpu.CompilerParams(vmem_limit_bytes=56 * MIB),
    )(queries, positions[None], new_keys)
    got = lax.all_to_all(message, ("x", "y"), 0, 0)
    kept = pl.pallas_call(
        slab_kernel,
        out_shape=jax.ShapeDtypeStruct(queue.shape, BF),
        in_specs=[ANY, ANY],
        out_specs=ANY,
        scratch_shapes=[pltpu.SemaphoreType.DMA],
        compiler_params=pltpu.CompilerParams(vmem_limit_bytes=56 * MIB),
        cost_estimate=LATE,
    )(message, queue)
    slab_keys, kept = lax.optimization_barrier((queue, kept))
    other = lax.ppermute(slab_keys, "c", swap)

    plane_keys = pl.pallas_call(
        lambda *refs: plane_keys_kernel(nq, *refs),
        out_shape=jax.ShapeDtypeStruct((srcs * nk, width), BF),
        in_specs=[VMEM],
        out_specs=VMEM,
        compiler_params=pltpu.CompilerParams(vmem_limit_bytes=4 * MIB),
        cost_estimate=EARLY,
    )(got)
    pairs = []
    for s in range(srcs):
        for c in range(2):
            for k in range(nz):
                to = (k + s) % nz if c == 0 else (k - s) % nz
                pairs.append(((s * 2 + c) * nz + k, (s * 2 + c) * nz + to))
    moved = lax.ppermute(plane_keys, ("x", "y", "c", "z"), pairs)

    owner = (step[0] % (srcs * 2)) == slab_index
    info = jnp.stack([slab_index * slab, (slab_index ^ 1) * slab, owner.astype(jnp.int32), core, z]).astype(jnp.int32)
    n = srcs * nq
    at = 2 * nq
    flops = 2 * n * 2 * slab * width
    out_shape = jax.ShapeDtypeStruct((srcs, at + srcs * nk + 8, width), BF)
    out = pl.pallas_call(
        lambda *refs: partial_kernel(scale, srcs, nq, *refs),
        out_shape=out_shape,
        in_specs=[SMEM, VMEM, VMEM, VMEM, ANY],
        out_specs=VMEM,
        scratch_shapes=[pltpu.VMEM((n, width), BF), pltpu.VMEM((n, 2 * slab), F32)],
        compiler_params=pltpu.CompilerParams(vmem_limit_bytes=24 * MIB),
        cost_estimate=pl.CostEstimate(flops=3 * flops, bytes_accessed=4 * slab * width, transcendentals=2 * n * slab),
    )(info, got, queue, other, plane_keys)
    out = pl.pallas_call(
        lambda *refs: fill_kernel(srcs, at, *refs),
        out_shape=out_shape,
        in_specs=[VMEM, VMEM],
        out_specs=VMEM,
        input_output_aliases={1: 0},
        compiler_params=pltpu.CompilerParams(vmem_limit_bytes=8 * MIB),
    )(moved, out)
    back = lax.all_to_all(out, ("x", "y"), 0, 0)
    twin = lax.ppermute(back[:, at:at + srcs * nk, :], "c", swap)

    loss, grad = pl.pallas_call(
        lambda *refs: combine_kernel(scale, srcs, nq, *refs),
        out_shape=(jax.ShapeDtypeStruct((1, nq), F32), jax.ShapeDtypeStruct((nq, width), BF)),
        in_specs=[VMEM, VMEM],
        out_specs=(VMEM, VMEM),
        compiler_params=pltpu.CompilerParams(vmem_limit_bytes=8 * MIB),
    )(back, queries)
    losses = loss.reshape(nq)

    updated = pl.pallas_call(
        lambda *refs: place_kernel(at, *refs),
        out_shape=jax.ShapeDtypeStruct(queue.shape, BF),
        in_specs=[SMEM, VMEM, VMEM, ANY],
        out_specs=ANY,
        scratch_shapes=[pltpu.VMEM(queue.shape, BF), pltpu.SemaphoreType.DMA],
        input_output_aliases={3: 0},
        compiler_params=pltpu.CompilerParams(vmem_limit_bytes=12 * MIB),
    )(info, back, twin, kept)
    return losses, grad, updated


def solution(mesh):
    gx, gy = mesh.devices.shape
    side = math.isqrt(gx // 2)
    fine = Mesh(np.asarray(mesh.devices).reshape(side, side, 2, gy), ("x", "y", "c", "z"))
    every = ("x", "y", "c", "z")
    return jax.shard_map(
        local,
        mesh=fine,
        in_specs=(P(every, None), P(every), P(("x", "y", "c"), None), P(every, None), P()),
        out_specs=(P(every), P(every, None), P(("x", "y", "c"), None)),
        check_vma=False,
    )
```

```python
import math

import jax
import jax.numpy as jnp
import numpy as np
from jax import lax
from jax.experimental import pallas as pl
from jax.experimental.pallas import tpu as pltpu
from jax.sharding import Mesh, PartitionSpec as P

BF = jnp.bfloat16
F32 = jnp.float32
ROWS = 40
MIB = 1024 * 1024
LOG2E = 1.4426950408889634
VMEM = pl.BlockSpec(memory_space=pltpu.VMEM)
ANY = pl.BlockSpec(memory_space=pl.ANY)
LATE = pl.CostEstimate(flops=6 * 10**9, bytes_accessed=0, transcendentals=0)
EARLY = pl.CostEstimate(flops=92 * 10**8, bytes_accessed=0, transcendentals=0)
SMEM = pl.BlockSpec(memory_space=pltpu.SMEM)


def rows_dot(a, b):
    return lax.dot_general(a, b, (((1,), (1,)), ((), ())), preferred_element_type=F32)


def partial_kernel(scale, srcs, nq, info_ref, msg_ref, own_ref, *refs):
    other_ref, _, out_ref, q_ref, s_ref = refs
    width = own_ref.shape[1]
    slab = own_ref.shape[0]
    n = srcs * nq
    block = 256
    lane = lax.broadcasted_iota(jnp.int32, (nq, width), 1)
    row = lax.broadcasted_iota(jnp.int32, (nq, width), 0)
    parts = []
    for j in range(srcs):
        q_ref[j * nq:(j + 1) * nq, :] = msg_ref[j, :nq, :]
        tail = msg_ref[j, nq:, :].astype(F32)
        line = tail[4:5, :] * 256.0 + tail[5:6, :]
        parts.append(jnp.sum(jnp.where(lane == row, line, 0.0), axis=1, keepdims=True))
    target = jnp.concatenate(parts, axis=0).astype(jnp.int32)
    queries = q_ref[...]
    top = None
    blocks = []
    for b in range(slab // block):
        blocks.append((info_ref[0] + b * block, own_ref, b))
    for b in range(slab // block):
        blocks.append((info_ref[1] + b * block, other_ref, b))
    for i, (start, ref, b) in enumerate(blocks):
        s = rows_dot(queries, ref[b * block:(b + 1) * block, :])
        s_ref[:, i * block:(i + 1) * block] = s
        for c in range(block // 128):
            piece = s[:, c * 128:(c + 1) * 128]
            top = piece if top is None else jnp.maximum(top, piece)
    point = jnp.max(top, axis=1, keepdims=True).astype(BF).astype(F32)
    total = jnp.zeros((n, 128), F32)
    grad = jnp.zeros((n, width), F32)
    positive = jnp.zeros((n, width), F32)
    column = lax.broadcasted_iota(jnp.int32, (n, block), 1)
    for i, (start, ref, b) in enumerate(blocks):
        s = s_ref[:, i * block:(i + 1) * block]
        hit = column == (target - start)
        e = jnp.where(hit, 0.0, jnp.exp2((s - point) * (scale * LOG2E)))
        for c in range(block // 128):
            total += e[:, c * 128:(c + 1) * 128]
        keys = ref[b * block:(b + 1) * block, :]
        grad += jnp.dot(e.astype(BF), keys, preferred_element_type=F32)
        positive += jnp.dot(hit.astype(F32).astype(BF), keys, preferred_element_type=F32)
    total = jnp.sum(total, axis=1, keepdims=True)
    t0 = total.astype(BF).astype(F32)
    t1 = (total - t0).astype(BF).astype(F32)
    t2 = total - t0 - t1
    stats = (point, t0, t1, t2)
    grad = grad.astype(BF)
    positive = positive.astype(BF)
    for j in range(srcs):
        at = slice(j * nq, (j + 1) * nq)
        out_ref[j, :nq, :] = grad[at]
        out_ref[j, nq:2 * nq, :] = positive[at]
    lane = lax.broadcasted_iota(jnp.int32, (nq, width), 1)
    row = lax.broadcasted_iota(jnp.int32, (nq, width), 0)
    for j in range(srcs):
        at = slice(j * nq, (j + 1) * nq)
        line = jnp.zeros((nq, width), F32)
        for k, value in enumerate(stats):
            line = jnp.where(lane == row + k * nq, value[at], line)
        line = jnp.sum(line, axis=0, keepdims=True)
        out_ref[j, out_ref.shape[1] - 8:, :] = jnp.broadcast_to(line, (8, width)).astype(BF)


def combine_kernel(scale, srcs, nq, got_ref, q_ref, loss_ref, grad_ref):
    width = q_ref.shape[1]
    lane = lax.broadcasted_iota(jnp.int32, (nq, 128), 1)
    row = lax.broadcasted_iota(jnp.int32, (nq, 128), 0)
    positive = jnp.zeros((nq, width), F32)
    points, totals = [], []
    for j in range(srcs):
        positive += got_ref[j, nq:2 * nq, :].astype(F32)
        st = jnp.broadcast_to(got_ref[j, got_ref.shape[1] - 8:, :].astype(F32)[:1, :128], (nq, 128))
        points.append(jnp.sum(jnp.where(lane == row, st, 0.0), axis=1, keepdims=True))
        three = (lane >= nq) & (lane % nq == row)
        totals.append(jnp.sum(jnp.where(three, st, 0.0), axis=1, keepdims=True))
    s_pos = jnp.sum(q_ref[...].astype(F32) * positive, axis=1, keepdims=True)
    top = s_pos
    for p in points:
        top = jnp.maximum(top, p)
    total = jnp.exp2((s_pos - top) * (scale * LOG2E))
    grad = jnp.zeros((nq, width), F32)
    for j in range(srcs):
        a = jnp.exp2((points[j] - top) * (scale * LOG2E))
        total += a * totals[j]
        grad += a * got_ref[j, :nq, :].astype(F32)
    log_total = jnp.log(total)
    lse = top * scale + log_total
    weight = (jnp.exp(s_pos * scale - lse) - 1.0).astype(BF).astype(F32)
    grad_ref[...] = ((grad / total + weight * positive) * scale).astype(BF)
    loss = lse - s_pos * scale
    loss_ref[...] = jnp.sum(jnp.where(lane == row, loss, 0.0), axis=0, keepdims=True)[:, :nq]


def message_kernel(copies, q_ref, pos_ref, keys_ref, out_ref, tail_ref):
    nq, nk = q_ref.shape[0], keys_ref.shape[0]
    tail_ref[...] = jnp.zeros_like(tail_ref)
    tail_ref[:nk, :] = keys_ref[...].astype(F32)
    tail_ref[nk:nk + 1, :nq] = (pos_ref[...] >> 8).astype(F32)
    tail_ref[nk + 1:nk + 2, :nq] = (pos_ref[...] & 255).astype(F32)
    tail = tail_ref[...].astype(BF)
    for j in range(copies):
        out_ref[j, :nq, :] = q_ref[...]
        out_ref[j, nq:, :] = tail


def fill_kernel(copies, at, keys_ref, in_ref, out_ref):
    del in_ref
    keys = keys_ref[...]
    for j in range(copies):
        out_ref[j, at:at + keys.shape[0], :] = keys


def slab_kernel(after_ref, queue_ref, out_ref, sem):
    del after_ref
    copy = pltpu.make_async_copy(queue_ref, out_ref, sem)
    copy.start()
    copy.wait()


def plane_keys_kernel(nq, got_ref, out_ref):
    width = out_ref.shape[1]
    row = lax.broadcasted_iota(jnp.int32, (8, width), 0)
    for a in range(got_ref.shape[0] // 4):
        t = [got_ref[4 * a + k, nq:, :].astype(F32)[:8] for k in range(4)]
        up = jnp.where(row < 4, t[0], pltpu.roll(t[1], 4, 0))
        down = jnp.where(row < 4, t[2], pltpu.roll(t[3], 4, 0))
        out_ref[16 * a:16 * a + 16, :] = jnp.concatenate([up, down], axis=0).astype(BF)


def place_kernel(at, info_ref, mine_ref, twin_ref, queue_ref, out_ref, new_ref, sem):
    del queue_ref
    owner, core, z = info_ref[2], info_ref[3], info_ref[4]
    cols, rows = twin_ref.shape[0], twin_ref.shape[1]
    width = twin_ref.shape[2]

    def put(ref, base, c):
        row = lax.broadcasted_iota(jnp.int32, (8, width), 0)
        for a in range(rows // 16):
            for b in range(4):
                tiles = []
                for k in range(4):
                    plane = 4 * b + k
                    slot = ((z - plane) if c == 0 else (plane - z)) & (cols - 1)
                    block = ref[slot, base + 16 * a:base + 16 * a + 16, :].astype(F32)
                    tiles.append((block[:8], block[8:]))
                for v in range(4):
                    t = [tiles[k][v // 2] for k in range(4)]
                    if v % 2 == 0:
                        up = jnp.where(row < 4, t[0], pltpu.roll(t[1], 4, 0))
                        down = jnp.where(row < 4, t[2], pltpu.roll(t[3], 4, 0))
                    else:
                        up = jnp.where(row < 4, pltpu.roll(t[0], 4, 0), t[1])
                        down = jnp.where(row < 4, pltpu.roll(t[2], 4, 0), t[3])
                    chip = 4 * a + v
                    start = (chip * 2 + c) * 64 + 16 * b
                    new_ref[start:start + 16, :] = jnp.concatenate([up, down], axis=0).astype(BF)

    for mine in (0, 1):
        @pl.when((owner == 1) & (core == mine))
        def _():
            put(mine_ref, at, mine)
            put(twin_ref, 0, 1 - mine)

    @pl.when(owner == 1)
    def _():
        copy = pltpu.make_async_copy(new_ref, out_ref, sem)
        copy.start()
        copy.wait()


def local(queries, positions, queue, new_keys, step):
    nq, width = queries.shape
    slab = queue.shape[0]
    nk = new_keys.shape[0]
    nz = lax.axis_size("z")
    srcs = lax.axis_size("x") * lax.axis_size("y")
    scale = 2.0 / math.sqrt(width)
    chip = lax.axis_index(("x", "y"))
    core = lax.axis_index("c")
    z = lax.axis_index("z")
    slab_index = chip * 2 + core
    swap = [(0, 1), (1, 0)]

    message = pl.pallas_call(
        lambda *refs: message_kernel(srcs, *refs),
        out_shape=jax.ShapeDtypeStruct((srcs, ROWS, width), BF),
        in_specs=[VMEM] * 3,
        out_specs=VMEM,
        scratch_shapes=[pltpu.VMEM((ROWS - nq, width), F32)],
        compiler_params=pltpu.CompilerParams(vmem_limit_bytes=56 * MIB),
    )(queries, positions[None], new_keys)
    got = lax.all_to_all(message, ("x", "y"), 0, 0)
    kept = pl.pallas_call(
        slab_kernel,
        out_shape=jax.ShapeDtypeStruct(queue.shape, BF),
        in_specs=[ANY, VMEM],
        out_specs=ANY,
        scratch_shapes=[pltpu.SemaphoreType.DMA],
        compiler_params=pltpu.CompilerParams(vmem_limit_bytes=56 * MIB),
        cost_estimate=LATE,
    )(message, queue)
    slab_keys, kept = lax.optimization_barrier((queue, kept))
    other = lax.ppermute(slab_keys, "c", swap)

    plane_keys = pl.pallas_call(
        lambda *refs: plane_keys_kernel(nq, *refs),
        out_shape=jax.ShapeDtypeStruct((srcs * nk, width), BF),
        in_specs=[VMEM],
        out_specs=VMEM,
        compiler_params=pltpu.CompilerParams(vmem_limit_bytes=4 * MIB),
        cost_estimate=EARLY,
    )(got)
    pairs = []
    for s in range(srcs):
        for c in range(2):
            for k in range(nz):
                to = (k + s) % nz if c == 0 else (k - s) % nz
                pairs.append(((s * 2 + c) * nz + k, (s * 2 + c) * nz + to))
    moved = lax.ppermute(plane_keys, ("x", "y", "c", "z"), pairs)

    owner = (step[0] % (srcs * 2)) == slab_index
    info = jnp.stack([slab_index * slab, (slab_index ^ 1) * slab, owner.astype(jnp.int32), core, z]).astype(jnp.int32)
    n = srcs * nq
    at = 2 * nq
    flops = 2 * n * 2 * slab * width
    out_shape = jax.ShapeDtypeStruct((srcs, at + srcs * nk + 8, width), BF)
    out = pl.pallas_call(
        lambda *refs: partial_kernel(scale, srcs, nq, *refs),
        out_shape=out_shape,
        in_specs=[SMEM, VMEM, VMEM, VMEM, ANY],
        out_specs=VMEM,
        scratch_shapes=[pltpu.VMEM((n, width), BF), pltpu.VMEM((n, 2 * slab), F32)],
        compiler_params=pltpu.CompilerParams(vmem_limit_bytes=24 * MIB),
        cost_estimate=pl.CostEstimate(flops=3 * flops, bytes_accessed=4 * slab * width, transcendentals=2 * n * slab),
    )(info, got, queue, other, plane_keys)
    out = pl.pallas_call(
        lambda *refs: fill_kernel(srcs, at, *refs),
        out_shape=out_shape,
        in_specs=[VMEM, VMEM],
        out_specs=VMEM,
        input_output_aliases={1: 0},
        compiler_params=pltpu.CompilerParams(vmem_limit_bytes=8 * MIB),
    )(moved, out)
    back = lax.all_to_all(out, ("x", "y"), 0, 0)
    twin = lax.ppermute(back[:, at:at + srcs * nk, :], "c", swap)

    loss, grad = pl.pallas_call(
        lambda *refs: combine_kernel(scale, srcs, nq, *refs),
        out_shape=(jax.ShapeDtypeStruct((1, nq), F32), jax.ShapeDtypeStruct((nq, width), BF)),
        in_specs=[VMEM, VMEM],
        out_specs=(VMEM, VMEM),
        compiler_params=pltpu.CompilerParams(vmem_limit_bytes=8 * MIB),
    )(back, queries)
    losses = loss.reshape(nq)

    updated = pl.pallas_call(
        lambda *refs: place_kernel(at, *refs),
        out_shape=jax.ShapeDtypeStruct(queue.shape, BF),
        in_specs=[SMEM, VMEM, VMEM, ANY],
        out_specs=ANY,
        scratch_shapes=[pltpu.VMEM(queue.shape, BF), pltpu.SemaphoreType.DMA],
        input_output_aliases={3: 0},
        compiler_params=pltpu.CompilerParams(vmem_limit_bytes=12 * MIB),
    )(info, back, twin, kept)
    return losses, grad, updated


def solution(mesh):
    gx, gy = mesh.devices.shape
    side = math.isqrt(gx // 2)
    fine = Mesh(np.asarray(mesh.devices).reshape(side, side, 2, gy), ("x", "y", "c", "z"))
    every = ("x", "y", "c", "z")
    return jax.shard_map(
        local,
        mesh=fine,
        in_specs=(P(every, None), P(every), P(("x", "y", "c"), None), P(every, None), P()),
        out_specs=(P(every), P(every, None), P(("x", "y", "c"), None)),
        check_vma=False,
    )
```

```python
import math

import jax
import jax.numpy as jnp
import numpy as np
from jax import lax
from jax.experimental import pallas as pl
from jax.experimental.pallas import tpu as pltpu
from jax.sharding import Mesh, PartitionSpec as P

BF = jnp.bfloat16
F32 = jnp.float32
ROWS = 40
MIB = 1024 * 1024
LOG2E = 1.4426950408889634
VMEM = pl.BlockSpec(memory_space=pltpu.VMEM)
ANY = pl.BlockSpec(memory_space=pl.ANY)
LATE = pl.CostEstimate(flops=6 * 10**9, bytes_accessed=0, transcendentals=0)
EARLY = pl.CostEstimate(flops=92 * 10**8, bytes_accessed=0, transcendentals=0)
SMEM = pl.BlockSpec(memory_space=pltpu.SMEM)


def rows_dot(a, b):
    return lax.dot_general(a, b, (((1,), (1,)), ((), ())), preferred_element_type=F32)


def partial_kernel(scale, srcs, nq, info_ref, msg_ref, own_ref, *refs):
    other_ref, _, out_ref, q_ref, s_ref = refs
    width = own_ref.shape[1]
    slab = own_ref.shape[0]
    n = srcs * nq
    block = 256
    lane = lax.broadcasted_iota(jnp.int32, (nq, width), 1)
    row = lax.broadcasted_iota(jnp.int32, (nq, width), 0)
    parts = []
    for j in range(srcs):
        q_ref[j * nq:(j + 1) * nq, :] = msg_ref[j, :nq, :]
        tail = msg_ref[j, nq:, :].astype(F32)
        line = tail[4:5, :] * 256.0 + tail[5:6, :]
        parts.append(jnp.sum(jnp.where(lane == row, line, 0.0), axis=1, keepdims=True))
    target = jnp.concatenate(parts, axis=0).astype(jnp.int32)
    queries = q_ref[...]
    top = None
    blocks = []
    for b in range(slab // block):
        blocks.append((info_ref[0] + b * block, own_ref, b))
    for b in range(slab // block):
        blocks.append((info_ref[1] + b * block, other_ref, b))
    for i, (start, ref, b) in enumerate(blocks):
        s = rows_dot(queries, ref[b * block:(b + 1) * block, :])
        s_ref[:, i * block:(i + 1) * block] = s
        for c in range(block // 128):
            piece = s[:, c * 128:(c + 1) * 128]
            top = piece if top is None else jnp.maximum(top, piece)
    point = jnp.max(top, axis=1, keepdims=True).astype(BF).astype(F32)
    total = jnp.zeros((n, 128), F32)
    grad = jnp.zeros((n, width), F32)
    positive = jnp.zeros((n, width), F32)
    column = lax.broadcasted_iota(jnp.int32, (n, block), 1).astype(F32).astype(BF)
    zero, one = jnp.zeros((n, block), BF), jnp.ones((n, block), BF)
    for i, (start, ref, b) in enumerate(blocks):
        s = s_ref[:, i * block:(i + 1) * block]
        e = jnp.exp2((s - point) * (scale * LOG2E))
        for c in range(block // 128):
            total += e[:, c * 128:(c + 1) * 128]
        hit = column == jnp.broadcast_to((target - start).astype(F32), (n, block)).astype(BF)
        keys = ref[b * block:(b + 1) * block, :]
        grad += jnp.dot(jnp.where(hit, zero, e.astype(BF)), keys, preferred_element_type=F32)
        positive += jnp.dot(jnp.where(hit, one, zero), keys, preferred_element_type=F32)
    total = jnp.sum(total, axis=1, keepdims=True)
    t0 = total.astype(BF).astype(F32)
    t1 = (total - t0).astype(BF).astype(F32)
    t2 = total - t0 - t1
    stats = (point, t0, t1, t2)
    grad = grad.astype(BF)
    positive = positive.astype(BF)
    for j in range(srcs):
        at = slice(j * nq, (j + 1) * nq)
        out_ref[j, :nq, :] = grad[at]
        out_ref[j, nq:2 * nq, :] = positive[at]
    lane = lax.broadcasted_iota(jnp.int32, (nq, width), 1)
    row = lax.broadcasted_iota(jnp.int32, (nq, width), 0)
    for j in range(srcs):
        at = slice(j * nq, (j + 1) * nq)
        line = jnp.zeros((nq, width), F32)
        for k, value in enumerate(stats):
            line = jnp.where(lane == row + k * nq, value[at], line)
        line = jnp.sum(line, axis=0, keepdims=True)
        out_ref[j, out_ref.shape[1] - 8:, :] = jnp.broadcast_to(line, (8, width)).astype(BF)


def combine_kernel(scale, srcs, nq, got_ref, q_ref, loss_ref, grad_ref):
    width = q_ref.shape[1]
    lane = lax.broadcasted_iota(jnp.int32, (nq, 128), 1)
    row = lax.broadcasted_iota(jnp.int32, (nq, 128), 0)
    positive = jnp.zeros((nq, width), F32)
    points, totals = [], []
    for j in range(srcs):
        positive += got_ref[j, nq:2 * nq, :].astype(F32)
        st = jnp.broadcast_to(got_ref[j, got_ref.shape[1] - 8:, :].astype(F32)[:1, :128], (nq, 128))
        points.append(jnp.sum(jnp.where(lane == row, st, 0.0), axis=1, keepdims=True))
        three = (lane >= nq) & (lane % nq == row)
        totals.append(jnp.sum(jnp.where(three, st, 0.0), axis=1, keepdims=True))
    s_pos = rows_dot(q_ref[...], positive.astype(BF))
    square = lax.broadcasted_iota(jnp.int32, (nq, nq), 0) == lax.broadcasted_iota(jnp.int32, (nq, nq), 1)
    s_pos = jnp.sum(jnp.where(square, s_pos, 0.0), axis=1, keepdims=True)
    top = s_pos
    for p in points:
        top = jnp.maximum(top, p)
    total = jnp.zeros((nq, 1), F32)
    grad = jnp.zeros((nq, width), F32)
    for j in range(srcs):
        a = jnp.exp2((points[j] - top) * (scale * LOG2E))
        total += a * totals[j]
        grad += a * got_ref[j, :nq, :].astype(F32)
    log_total = jnp.log(total)
    lse = top * scale + log_total
    weight = (jnp.exp(s_pos * scale - lse) - 1.0).astype(BF).astype(F32)
    grad_ref[...] = ((grad / total + weight * positive) * scale).astype(BF)
    loss = lse - s_pos * scale
    loss_ref[...] = jnp.sum(jnp.where(lane == row, loss, 0.0), axis=0, keepdims=True)[:, :nq]


def message_kernel(copies, q_ref, pos_ref, keys_ref, out_ref, tail_ref):
    nq, nk = q_ref.shape[0], keys_ref.shape[0]
    tail_ref[...] = jnp.zeros_like(tail_ref)
    tail_ref[:nk, :] = keys_ref[...].astype(F32)
    tail_ref[nk:nk + 1, :nq] = (pos_ref[...] >> 8).astype(F32)
    tail_ref[nk + 1:nk + 2, :nq] = (pos_ref[...] & 255).astype(F32)
    tail = tail_ref[...].astype(BF)
    for j in range(copies):
        out_ref[j, :nq, :] = q_ref[...]
        out_ref[j, nq:, :] = tail


def fill_kernel(copies, at, keys_ref, in_ref, out_ref):
    del in_ref
    keys = keys_ref[...]
    for j in range(copies):
        out_ref[j, at:at + keys.shape[0], :] = keys


def slab_kernel(after_ref, queue_ref, out_ref, sem):
    del after_ref
    copy = pltpu.make_async_copy(queue_ref, out_ref, sem)
    copy.start()
    copy.wait()


def plane_keys_kernel(nq, got_ref, out_ref):
    width = out_ref.shape[1]
    row = lax.broadcasted_iota(jnp.int32, (8, width), 0)
    for a in range(got_ref.shape[0] // 4):
        t = [got_ref[4 * a + k, nq:, :].astype(F32)[:8] for k in range(4)]
        up = jnp.where(row < 4, t[0], pltpu.roll(t[1], 4, 0))
        down = jnp.where(row < 4, t[2], pltpu.roll(t[3], 4, 0))
        out_ref[16 * a:16 * a + 16, :] = jnp.concatenate([up, down], axis=0).astype(BF)


def place_kernel(at, info_ref, mine_ref, twin_ref, queue_ref, out_ref, new_ref, sem):
    del queue_ref
    owner, core, z = info_ref[2], info_ref[3], info_ref[4]
    cols, rows = twin_ref.shape[0], twin_ref.shape[1]
    width = twin_ref.shape[2]

    def put(ref, base, c):
        row = lax.broadcasted_iota(jnp.int32, (8, width), 0)
        for a in range(rows // 16):
            for b in range(4):
                tiles = []
                for k in range(4):
                    plane = 4 * b + k
                    slot = ((z - plane) if c == 0 else (plane - z)) & (cols - 1)
                    block = ref[slot, base + 16 * a:base + 16 * a + 16, :].astype(F32)
                    tiles.append((block[:8], block[8:]))
                for v in range(4):
                    t = [tiles[k][v // 2] for k in range(4)]
                    if v % 2 == 0:
                        up = jnp.where(row < 4, t[0], pltpu.roll(t[1], 4, 0))
                        down = jnp.where(row < 4, t[2], pltpu.roll(t[3], 4, 0))
                    else:
                        up = jnp.where(row < 4, pltpu.roll(t[0], 4, 0), t[1])
                        down = jnp.where(row < 4, pltpu.roll(t[2], 4, 0), t[3])
                    chip = 4 * a + v
                    start = (chip * 2 + c) * 64 + 16 * b
                    new_ref[start:start + 16, :] = jnp.concatenate([up, down], axis=0).astype(BF)

    for mine in (0, 1):
        @pl.when((owner == 1) & (core == mine))
        def _():
            put(mine_ref, at, mine)
            put(twin_ref, 0, 1 - mine)

    @pl.when(owner == 1)
    def _():
        copy = pltpu.make_async_copy(new_ref, out_ref, sem)
        copy.start()
        copy.wait()


def local(queries, positions, queue, new_keys, step):
    nq, width = queries.shape
    slab = queue.shape[0]
    nk = new_keys.shape[0]
    nz = lax.axis_size("z")
    srcs = lax.axis_size("x") * lax.axis_size("y")
    scale = 2.0 / math.sqrt(width)
    chip = lax.axis_index(("x", "y"))
    core = lax.axis_index("c")
    z = lax.axis_index("z")
    slab_index = chip * 2 + core
    swap = [(0, 1), (1, 0)]

    message = pl.pallas_call(
        lambda *refs: message_kernel(srcs, *refs),
        out_shape=jax.ShapeDtypeStruct((srcs, ROWS, width), BF),
        in_specs=[VMEM] * 3,
        out_specs=VMEM,
        scratch_shapes=[pltpu.VMEM((ROWS - nq, width), F32)],
        compiler_params=pltpu.CompilerParams(vmem_limit_bytes=56 * MIB),
    )(queries, positions[None], new_keys)
    got = lax.all_to_all(message, ("x", "y"), 0, 0)
    kept = pl.pallas_call(
        slab_kernel,
        out_shape=jax.ShapeDtypeStruct(queue.shape, BF),
        in_specs=[ANY, VMEM],
        out_specs=ANY,
        scratch_shapes=[pltpu.SemaphoreType.DMA],
        compiler_params=pltpu.CompilerParams(vmem_limit_bytes=56 * MIB),
        cost_estimate=LATE,
    )(message, queue)
    slab_keys, kept = lax.optimization_barrier((queue, kept))
    other = lax.ppermute(slab_keys, "c", swap)

    plane_keys = pl.pallas_call(
        lambda *refs: plane_keys_kernel(nq, *refs),
        out_shape=jax.ShapeDtypeStruct((srcs * nk, width), BF),
        in_specs=[VMEM],
        out_specs=VMEM,
        compiler_params=pltpu.CompilerParams(vmem_limit_bytes=4 * MIB),
        cost_estimate=EARLY,
    )(got)
    pairs = []
    for s in range(srcs):
        for c in range(2):
            for k in range(nz):
                to = (k + s) % nz if c == 0 else (k - s) % nz
                pairs.append(((s * 2 + c) * nz + k, (s * 2 + c) * nz + to))
    moved = lax.ppermute(plane_keys, ("x", "y", "c", "z"), pairs)

    owner = (step[0] % (srcs * 2)) == slab_index
    info = jnp.stack([slab_index * slab, (slab_index ^ 1) * slab, owner.astype(jnp.int32), core, z]).astype(jnp.int32)
    n = srcs * nq
    at = 2 * nq
    flops = 2 * n * 2 * slab * width
    out_shape = jax.ShapeDtypeStruct((srcs, at + srcs * nk + 8, width), BF)
    out = pl.pallas_call(
        lambda *refs: partial_kernel(scale, srcs, nq, *refs),
        out_shape=out_shape,
        in_specs=[SMEM, VMEM, VMEM, VMEM, ANY],
        out_specs=VMEM,
        scratch_shapes=[pltpu.VMEM((n, width), BF), pltpu.VMEM((n, 2 * slab), F32)],
        compiler_params=pltpu.CompilerParams(vmem_limit_bytes=24 * MIB),
        cost_estimate=pl.CostEstimate(flops=3 * flops, bytes_accessed=4 * slab * width, transcendentals=2 * n * slab),
    )(info, got, queue, other, plane_keys)
    out = pl.pallas_call(
        lambda *refs: fill_kernel(srcs, at, *refs),
        out_shape=out_shape,
        in_specs=[VMEM, VMEM],
        out_specs=VMEM,
        input_output_aliases={1: 0},
        compiler_params=pltpu.CompilerParams(vmem_limit_bytes=8 * MIB),
    )(moved, out)
    back = lax.all_to_all(out, ("x", "y"), 0, 0)
    twin = lax.ppermute(back[:, at:at + srcs * nk, :], "c", swap)

    loss, grad = pl.pallas_call(
        lambda *refs: combine_kernel(scale, srcs, nq, *refs),
        out_shape=(jax.ShapeDtypeStruct((1, nq), F32), jax.ShapeDtypeStruct((nq, width), BF)),
        in_specs=[VMEM, VMEM],
        out_specs=(VMEM, VMEM),
        compiler_params=pltpu.CompilerParams(vmem_limit_bytes=8 * MIB),
    )(back, queries)
    losses = loss.reshape(nq)

    updated = pl.pallas_call(
        lambda *refs: place_kernel(at, *refs),
        out_shape=jax.ShapeDtypeStruct(queue.shape, BF),
        in_specs=[SMEM, VMEM, VMEM, ANY],
        out_specs=ANY,
        scratch_shapes=[pltpu.VMEM(queue.shape, BF), pltpu.SemaphoreType.DMA],
        input_output_aliases={3: 0},
        compiler_params=pltpu.CompilerParams(vmem_limit_bytes=12 * MIB),
    )(info, back, twin, kept)
    return losses, grad, updated


def solution(mesh):
    gx, gy = mesh.devices.shape
    side = math.isqrt(gx // 2)
    fine = Mesh(np.asarray(mesh.devices).reshape(side, side, 2, gy), ("x", "y", "c", "z"))
    every = ("x", "y", "c", "z")
    return jax.shard_map(
        local,
        mesh=fine,
        in_specs=(P(every, None), P(every), P(("x", "y", "c"), None), P(every, None), P()),
        out_specs=(P(every), P(every, None), P(("x", "y", "c"), None)),
        check_vma=False,
    )
```

```python
import math

import jax
import jax.numpy as jnp
import numpy as np
from jax import lax
from jax.experimental import pallas as pl
from jax.experimental.pallas import tpu as pltpu
from jax.sharding import Mesh, PartitionSpec as P

BF = jnp.bfloat16
F32 = jnp.float32
ROWS = 40
MIB = 1024 * 1024
LOG2E = 1.4426950408889634
VMEM = pl.BlockSpec(memory_space=pltpu.VMEM)
ANY = pl.BlockSpec(memory_space=pl.ANY)
LATE = pl.CostEstimate(flops=6 * 10**9, bytes_accessed=0, transcendentals=0)
EARLY = pl.CostEstimate(flops=92 * 10**8, bytes_accessed=0, transcendentals=0)
SMEM = pl.BlockSpec(memory_space=pltpu.SMEM)


def rows_dot(a, b):
    return lax.dot_general(a, b, (((1,), (1,)), ((), ())), preferred_element_type=F32)


def partial_kernel(scale, srcs, nq, info_ref, msg_ref, own_ref, *refs):
    other_ref, _, out_ref, q_ref, s_ref = refs
    width = own_ref.shape[1]
    slab = own_ref.shape[0]
    n = srcs * nq
    block = 256
    lane = lax.broadcasted_iota(jnp.int32, (nq, width), 1)
    row = lax.broadcasted_iota(jnp.int32, (nq, width), 0)
    parts = []
    for j in range(srcs):
        q_ref[j * nq:(j + 1) * nq, :] = msg_ref[j, :nq, :]
        tail = msg_ref[j, nq:, :].astype(F32)
        line = tail[4:5, :] * 256.0 + tail[5:6, :]
        parts.append(jnp.sum(jnp.where(lane == row, line, 0.0), axis=1, keepdims=True))
    target = jnp.concatenate(parts, axis=0).astype(jnp.int32)
    queries = q_ref[...]
    top = None
    blocks = []
    for b in range(slab // block):
        blocks.append((info_ref[0] + b * block, own_ref, b))
    for b in range(slab // block):
        blocks.append((info_ref[1] + b * block, other_ref, b))
    for i, (start, ref, b) in enumerate(blocks):
        s = rows_dot(queries, ref[b * block:(b + 1) * block, :])
        s_ref[:, i * block:(i + 1) * block] = s
        for c in range(block // 128):
            piece = s[:, c * 128:(c + 1) * 128]
            top = piece if top is None else jnp.maximum(top, piece)
    point = jnp.max(top, axis=1, keepdims=True).astype(BF).astype(F32)
    total = jnp.zeros((n, 128), F32)
    grad = jnp.zeros((n, width), F32)
    positive = jnp.zeros((n, width), F32)
    column = lax.broadcasted_iota(jnp.int32, (n, block), 1).astype(F32).astype(BF)
    zero, one = jnp.zeros((n, block), BF), jnp.ones((n, block), BF)
    for i, (start, ref, b) in enumerate(blocks):
        s = s_ref[:, i * block:(i + 1) * block]
        e = jnp.exp2((s - point) * (scale * LOG2E))
        for c in range(block // 128):
            total += e[:, c * 128:(c + 1) * 128]
        hit = column == jnp.broadcast_to((target - start).astype(F32), (n, block)).astype(BF)
        keys = ref[b * block:(b + 1) * block, :]
        grad += jnp.dot(jnp.where(hit, zero, e.astype(BF)), keys, preferred_element_type=F32)
        positive += jnp.dot(jnp.where(hit, one, zero), keys, preferred_element_type=F32)
    total = jnp.sum(total, axis=1, keepdims=True)
    t0 = total.astype(BF).astype(F32)
    t1 = (total - t0).astype(BF).astype(F32)
    t2 = total - t0 - t1
    stats = (point, t0, t1, t2)
    grad = grad.astype(BF)
    positive = positive.astype(BF)
    for j in range(srcs):
        at = slice(j * nq, (j + 1) * nq)
        out_ref[j, :nq, :] = grad[at]
        out_ref[j, nq:2 * nq, :] = positive[at]
    lane = lax.broadcasted_iota(jnp.int32, (nq, width), 1)
    row = lax.broadcasted_iota(jnp.int32, (nq, width), 0)
    for j in range(srcs):
        at = slice(j * nq, (j + 1) * nq)
        line = jnp.zeros((nq, width), F32)
        for k, value in enumerate(stats):
            line = jnp.where(lane == row + k * nq, value[at], line)
        line = jnp.sum(line, axis=0, keepdims=True)
        out_ref[j, out_ref.shape[1] - 8:, :] = jnp.broadcast_to(line, (8, width)).astype(BF)


def combine_kernel(scale, srcs, nq, got_ref, q_ref, loss_ref, grad_ref):
    width = q_ref.shape[1]
    lane = lax.broadcasted_iota(jnp.int32, (nq, 128), 1)
    row = lax.broadcasted_iota(jnp.int32, (nq, 128), 0)
    positive = jnp.zeros((nq, width), F32)
    points, totals = [], []
    for j in range(srcs):
        positive += got_ref[j, nq:2 * nq, :].astype(F32)
        st = jnp.broadcast_to(got_ref[j, got_ref.shape[1] - 8:, :].astype(F32)[:1, :128], (nq, 128))
        points.append(jnp.sum(jnp.where(lane == row, st, 0.0), axis=1, keepdims=True))
        three = (lane >= nq) & (lane % nq == row)
        totals.append(jnp.sum(jnp.where(three, st, 0.0), axis=1, keepdims=True))
    s_pos = rows_dot(q_ref[...], positive.astype(BF))
    square = lax.broadcasted_iota(jnp.int32, (nq, nq), 0) == lax.broadcasted_iota(jnp.int32, (nq, nq), 1)
    s_pos = jnp.sum(jnp.where(square, s_pos, 0.0), axis=1, keepdims=True)
    top = s_pos
    for p in points:
        top = jnp.maximum(top, p)
    total = jnp.zeros((nq, 1), F32)
    grad = jnp.zeros((nq, width), F32)
    for j in range(srcs):
        a = jnp.exp2((points[j] - top) * (scale * LOG2E))
        total += a * totals[j]
        grad += a * got_ref[j, :nq, :].astype(F32)
    log_total = jnp.log(total)
    lse = top * scale + log_total
    weight = (jnp.exp(s_pos * scale - lse) - 1.0).astype(BF).astype(F32)
    grad_ref[...] = ((grad / total + weight * positive) * scale).astype(BF)
    loss = lse - s_pos * scale
    loss_ref[...] = jnp.sum(jnp.where(lane == row, loss, 0.0), axis=0, keepdims=True)[:, :nq]


def message_kernel(copies, q_ref, pos_ref, keys_ref, out_ref, tail_ref):
    nq, nk = q_ref.shape[0], keys_ref.shape[0]
    tail_ref[...] = jnp.zeros_like(tail_ref)
    tail_ref[:nk, :] = keys_ref[...].astype(F32)
    tail_ref[nk:nk + 1, :nq] = (pos_ref[...] >> 8).astype(F32)
    tail_ref[nk + 1:nk + 2, :nq] = (pos_ref[...] & 255).astype(F32)
    tail = tail_ref[...].astype(BF)
    for j in range(copies):
        out_ref[j, :nq, :] = q_ref[...]
        out_ref[j, nq:, :] = tail


def fill_kernel(copies, at, keys_ref, in_ref, out_ref):
    del in_ref
    keys = keys_ref[...]
    for j in range(copies):
        out_ref[j, at:at + keys.shape[0], :] = keys


def slab_kernel(after_ref, queue_ref, out_ref, sem):
    del after_ref
    copy = pltpu.make_async_copy(queue_ref, out_ref, sem)
    copy.start()
    copy.wait()


def plane_keys_kernel(nq, got_ref, out_ref):
    width = out_ref.shape[1]
    row = lax.broadcasted_iota(jnp.int32, (8, width), 0)
    for a in range(got_ref.shape[0] // 4):
        t = [got_ref[4 * a + k, nq:, :].astype(F32)[:8] for k in range(4)]
        up = jnp.where(row < 4, t[0], pltpu.roll(t[1], 4, 0))
        down = jnp.where(row < 4, t[2], pltpu.roll(t[3], 4, 0))
        out_ref[16 * a:16 * a + 16, :] = jnp.concatenate([up, down], axis=0).astype(BF)


def place_kernel(at, info_ref, mine_ref, twin_ref, queue_ref, out_ref, new_ref, sem):
    del queue_ref
    owner, core, z = info_ref[2], info_ref[3], info_ref[4]
    cols, rows = twin_ref.shape[0], twin_ref.shape[1]
    width = twin_ref.shape[2]

    def put(ref, base, c):
        row = lax.broadcasted_iota(jnp.int32, (8, width), 0)
        for a in range(rows // 16):
            for b in range(4):
                tiles = []
                for k in range(4):
                    plane = 4 * b + k
                    slot = (z - plane - c * (cols // 2)) & (cols - 1)
                    block = ref[slot, base + 16 * a:base + 16 * a + 16, :].astype(F32)
                    tiles.append((block[:8], block[8:]))
                for v in range(4):
                    t = [tiles[k][v // 2] for k in range(4)]
                    if v % 2 == 0:
                        up = jnp.where(row < 4, t[0], pltpu.roll(t[1], 4, 0))
                        down = jnp.where(row < 4, t[2], pltpu.roll(t[3], 4, 0))
                    else:
                        up = jnp.where(row < 4, pltpu.roll(t[0], 4, 0), t[1])
                        down = jnp.where(row < 4, pltpu.roll(t[2], 4, 0), t[3])
                    chip = 4 * a + v
                    start = (chip * 2 + c) * 64 + 16 * b
                    new_ref[start:start + 16, :] = jnp.concatenate([up, down], axis=0).astype(BF)

    for mine in (0, 1):
        @pl.when((owner == 1) & (core == mine))
        def _():
            put(mine_ref, at, mine)
            put(twin_ref, 0, 1 - mine)

    @pl.when(owner == 1)
    def _():
        copy = pltpu.make_async_copy(new_ref, out_ref, sem)
        copy.start()
        copy.wait()


def local(queries, positions, queue, new_keys, step):
    nq, width = queries.shape
    slab = queue.shape[0]
    nk = new_keys.shape[0]
    nz = lax.axis_size("z")
    srcs = lax.axis_size("x") * lax.axis_size("y")
    scale = 2.0 / math.sqrt(width)
    chip = lax.axis_index(("x", "y"))
    core = lax.axis_index("c")
    z = lax.axis_index("z")
    slab_index = chip * 2 + core
    swap = [(0, 1), (1, 0)]

    message = pl.pallas_call(
        lambda *refs: message_kernel(srcs, *refs),
        out_shape=jax.ShapeDtypeStruct((srcs, ROWS, width), BF),
        in_specs=[VMEM] * 3,
        out_specs=VMEM,
        scratch_shapes=[pltpu.VMEM((ROWS - nq, width), F32)],
        compiler_params=pltpu.CompilerParams(vmem_limit_bytes=56 * MIB),
    )(queries, positions[None], new_keys)
    got = lax.all_to_all(message, ("x", "y"), 0, 0)
    kept = pl.pallas_call(
        slab_kernel,
        out_shape=jax.ShapeDtypeStruct(queue.shape, BF),
        in_specs=[ANY, VMEM],
        out_specs=ANY,
        scratch_shapes=[pltpu.SemaphoreType.DMA],
        compiler_params=pltpu.CompilerParams(vmem_limit_bytes=56 * MIB),
        cost_estimate=LATE,
    )(message, queue)
    slab_keys, kept = lax.optimization_barrier((queue, kept))
    other = lax.ppermute(slab_keys, "c", swap)

    plane_keys = pl.pallas_call(
        lambda *refs: plane_keys_kernel(nq, *refs),
        out_shape=jax.ShapeDtypeStruct((srcs * nk, width), BF),
        in_specs=[VMEM],
        out_specs=VMEM,
        compiler_params=pltpu.CompilerParams(vmem_limit_bytes=4 * MIB),
        cost_estimate=EARLY,
    )(got)
    pairs = []
    for s in range(srcs):
        for c in range(2):
            for k in range(nz):
                to = (k + s + c * nz // 2) % nz
                pairs.append(((s * 2 + c) * nz + k, (s * 2 + c) * nz + to))
    moved = lax.ppermute(plane_keys, ("x", "y", "c", "z"), pairs)

    owner = (step[0] % (srcs * 2)) == slab_index
    info = jnp.stack([slab_index * slab, (slab_index ^ 1) * slab, owner.astype(jnp.int32), core, z]).astype(jnp.int32)
    n = srcs * nq
    at = 2 * nq
    flops = 2 * n * 2 * slab * width
    out_shape = jax.ShapeDtypeStruct((srcs, at + srcs * nk + 8, width), BF)
    out = pl.pallas_call(
        lambda *refs: partial_kernel(scale, srcs, nq, *refs),
        out_shape=out_shape,
        in_specs=[SMEM, VMEM, VMEM, VMEM, ANY],
        out_specs=VMEM,
        scratch_shapes=[pltpu.VMEM((n, width), BF), pltpu.VMEM((n, 2 * slab), F32)],
        compiler_params=pltpu.CompilerParams(vmem_limit_bytes=24 * MIB),
        cost_estimate=pl.CostEstimate(flops=3 * flops, bytes_accessed=4 * slab * width, transcendentals=2 * n * slab),
    )(info, got, queue, other, plane_keys)
    out = pl.pallas_call(
        lambda *refs: fill_kernel(srcs, at, *refs),
        out_shape=out_shape,
        in_specs=[VMEM, VMEM],
        out_specs=VMEM,
        input_output_aliases={1: 0},
        compiler_params=pltpu.CompilerParams(vmem_limit_bytes=8 * MIB),
    )(moved, out)
    back = lax.all_to_all(out, ("x", "y"), 0, 0)
    twin = lax.ppermute(back[:, at:at + srcs * nk, :], "c", swap)

    loss, grad = pl.pallas_call(
        lambda *refs: combine_kernel(scale, srcs, nq, *refs),
        out_shape=(jax.ShapeDtypeStruct((1, nq), F32), jax.ShapeDtypeStruct((nq, width), BF)),
        in_specs=[VMEM, VMEM],
        out_specs=(VMEM, VMEM),
        compiler_params=pltpu.CompilerParams(vmem_limit_bytes=8 * MIB),
    )(back, queries)
    losses = loss.reshape(nq)

    updated = pl.pallas_call(
        lambda *refs: place_kernel(at, *refs),
        out_shape=jax.ShapeDtypeStruct(queue.shape, BF),
        in_specs=[SMEM, VMEM, VMEM, ANY],
        out_specs=ANY,
        scratch_shapes=[pltpu.VMEM(queue.shape, BF), pltpu.SemaphoreType.DMA],
        input_output_aliases={3: 0},
        compiler_params=pltpu.CompilerParams(vmem_limit_bytes=12 * MIB),
    )(info, back, twin, kept)
    return losses, grad, updated


def solution(mesh):
    gx, gy = mesh.devices.shape
    side = math.isqrt(gx // 2)
    fine = Mesh(np.asarray(mesh.devices).reshape(side, side, 2, gy), ("x", "y", "c", "z"))
    every = ("x", "y", "c", "z")
    return jax.shard_map(
        local,
        mesh=fine,
        in_specs=(P(every, None), P(every), P(("x", "y", "c"), None), P(every, None), P()),
        out_specs=(P(every), P(every, None), P(("x", "y", "c"), None)),
        check_vma=False,
    )
```

```python
import math

import jax
import jax.numpy as jnp
import numpy as np
from jax import lax
from jax.experimental import pallas as pl
from jax.experimental.pallas import tpu as pltpu
from jax.sharding import Mesh, PartitionSpec as P

BF = jnp.bfloat16
F32 = jnp.float32
ROWS = 40
MIB = 1024 * 1024
LOG2E = 1.4426950408889634
VMEM = pl.BlockSpec(memory_space=pltpu.VMEM)
ANY = pl.BlockSpec(memory_space=pl.ANY)
LATE = pl.CostEstimate(flops=6 * 10**9, bytes_accessed=0, transcendentals=0)
EARLY = pl.CostEstimate(flops=92 * 10**8, bytes_accessed=0, transcendentals=0)
SMEM = pl.BlockSpec(memory_space=pltpu.SMEM)


def rows_dot(a, b):
    return lax.dot_general(a, b, (((1,), (1,)), ((), ())), preferred_element_type=F32)


def partial_kernel(scale, srcs, nq, info_ref, msg_ref, own_ref, *refs):
    other_ref, _, out_ref, q_ref, s_ref = refs
    width = own_ref.shape[1]
    slab = own_ref.shape[0]
    n = srcs * nq
    block = 256
    lane = lax.broadcasted_iota(jnp.int32, (nq, width), 1)
    row = lax.broadcasted_iota(jnp.int32, (nq, width), 0)
    parts = []
    for j in range(srcs):
        q_ref[j * nq:(j + 1) * nq, :] = msg_ref[j, :nq, :]
        tail = msg_ref[j, nq:, :].astype(F32)
        line = tail[4:5, :] * 256.0 + tail[5:6, :]
        parts.append(jnp.sum(jnp.where(lane == row, line, 0.0), axis=1, keepdims=True))
    target = jnp.concatenate(parts, axis=0).astype(jnp.int32)
    blocks = []
    for b in range(slab // block):
        blocks.append((info_ref[0] + b * block, own_ref, b))
    for b in range(slab // block):
        blocks.append((info_ref[1] + b * block, other_ref, b))
    half = n // 2
    column = lax.broadcasted_iota(jnp.int32, (half, block), 1).astype(F32).astype(BF)
    zero, one = jnp.zeros((half, block), BF), jnp.ones((half, block), BF)

    def score(at, i, top):
        _, ref, b = blocks[i]
        s = rows_dot(q_ref[at, :], ref[b * block:(b + 1) * block, :])
        s_ref[at, i * block:(i + 1) * block] = s
        for c in range(block // 128):
            piece = s[:, c * 128:(c + 1) * 128]
            top = piece if top is None else jnp.maximum(top, piece)
        return top

    halves = (slice(0, half), slice(half, n))
    tops = [None, None]
    for i in range(len(blocks)):
        tops[0] = score(halves[0], i, tops[0])
    found = []
    for h, at in enumerate(halves):
        point = jnp.max(tops[h], axis=1, keepdims=True).astype(BF).astype(F32)
        total = jnp.zeros((half, 128), F32)
        grad = jnp.zeros((half, width), F32)
        positive = jnp.zeros((half, width), F32)
        for i, (start, ref, b) in enumerate(blocks):
            if h == 0:
                tops[1] = score(halves[1], i, tops[1])
            s = s_ref[at, i * block:(i + 1) * block]
            e = jnp.exp2((s - point) * (scale * LOG2E))
            for c in range(block // 128):
                total += e[:, c * 128:(c + 1) * 128]
            hit = column == jnp.broadcast_to((target[at] - start).astype(F32), (half, block)).astype(BF)
            keys = ref[b * block:(b + 1) * block, :]
            grad += jnp.dot(jnp.where(hit, zero, e.astype(BF)), keys, preferred_element_type=F32)
            positive += jnp.dot(jnp.where(hit, one, zero), keys, preferred_element_type=F32)
        found.append((point, total, grad, positive))
    point, total, grad, positive = (jnp.concatenate(pair, axis=0) for pair in zip(*found))
    total = jnp.sum(total, axis=1, keepdims=True)
    t0 = total.astype(BF).astype(F32)
    t1 = (total - t0).astype(BF).astype(F32)
    t2 = total - t0 - t1
    stats = (point, t0, t1, t2)
    grad = grad.astype(BF)
    positive = positive.astype(BF)
    for j in range(srcs):
        at = slice(j * nq, (j + 1) * nq)
        out_ref[j, :nq, :] = grad[at]
        out_ref[j, nq:2 * nq, :] = positive[at]
    lane = lax.broadcasted_iota(jnp.int32, (nq, width), 1)
    row = lax.broadcasted_iota(jnp.int32, (nq, width), 0)
    for j in range(srcs):
        at = slice(j * nq, (j + 1) * nq)
        line = jnp.zeros((nq, width), F32)
        for k, value in enumerate(stats):
            line = jnp.where(lane == row + k * nq, value[at], line)
        line = jnp.sum(line, axis=0, keepdims=True)
        out_ref[j, out_ref.shape[1] - 8:, :] = jnp.broadcast_to(line, (8, width)).astype(BF)


def combine_kernel(scale, srcs, nq, got_ref, q_ref, loss_ref, grad_ref):
    width = q_ref.shape[1]
    lane = lax.broadcasted_iota(jnp.int32, (nq, 128), 1)
    row = lax.broadcasted_iota(jnp.int32, (nq, 128), 0)
    positive = jnp.zeros((nq, width), F32)
    points, totals = [], []
    for j in range(srcs):
        positive += got_ref[j, nq:2 * nq, :].astype(F32)
        st = jnp.broadcast_to(got_ref[j, got_ref.shape[1] - 8:, :].astype(F32)[:1, :128], (nq, 128))
        points.append(jnp.sum(jnp.where(lane == row, st, 0.0), axis=1, keepdims=True))
        three = (lane >= nq) & (lane % nq == row)
        totals.append(jnp.sum(jnp.where(three, st, 0.0), axis=1, keepdims=True))
    s_pos = rows_dot(q_ref[...], positive.astype(BF))
    square = lax.broadcasted_iota(jnp.int32, (nq, nq), 0) == lax.broadcasted_iota(jnp.int32, (nq, nq), 1)
    s_pos = jnp.sum(jnp.where(square, s_pos, 0.0), axis=1, keepdims=True)
    top = s_pos
    for p in points:
        top = jnp.maximum(top, p)
    total = jnp.zeros((nq, 1), F32)
    grad = jnp.zeros((nq, width), F32)
    for j in range(srcs):
        a = jnp.exp2((points[j] - top) * (scale * LOG2E))
        total += a * totals[j]
        grad += a * got_ref[j, :nq, :].astype(F32)
    log_total = jnp.log(total)
    lse = top * scale + log_total
    weight = (jnp.exp(s_pos * scale - lse) - 1.0).astype(BF).astype(F32)
    grad_ref[...] = ((grad / total + weight * positive) * scale).astype(BF)
    loss = lse - s_pos * scale
    loss_ref[...] = jnp.sum(jnp.where(lane == row, loss, 0.0), axis=0, keepdims=True)[:, :nq]


def message_kernel(copies, q_ref, pos_ref, keys_ref, out_ref, tail_ref):
    nq, nk = q_ref.shape[0], keys_ref.shape[0]
    tail_ref[...] = jnp.zeros_like(tail_ref)
    tail_ref[:nk, :] = keys_ref[...].astype(F32)
    tail_ref[nk:nk + 1, :nq] = (pos_ref[...] >> 8).astype(F32)
    tail_ref[nk + 1:nk + 2, :nq] = (pos_ref[...] & 255).astype(F32)
    tail = tail_ref[...].astype(BF)
    for j in range(copies):
        out_ref[j, :nq, :] = q_ref[...]
        out_ref[j, nq:, :] = tail


def fill_kernel(copies, at, keys_ref, in_ref, out_ref):
    del in_ref
    keys = keys_ref[...]
    for j in range(copies):
        out_ref[j, at:at + keys.shape[0], :] = keys


def slab_kernel(after_ref, queue_ref, out_ref, sem):
    del after_ref
    copy = pltpu.make_async_copy(queue_ref, out_ref, sem)
    copy.start()
    copy.wait()


def plane_keys_kernel(nq, got_ref, out_ref):
    width = out_ref.shape[1]
    row = lax.broadcasted_iota(jnp.int32, (8, width), 0)
    for a in range(got_ref.shape[0] // 4):
        t = [got_ref[4 * a + k, nq:, :].astype(F32)[:8] for k in range(4)]
        up = jnp.where(row < 4, t[0], pltpu.roll(t[1], 4, 0))
        down = jnp.where(row < 4, t[2], pltpu.roll(t[3], 4, 0))
        out_ref[16 * a:16 * a + 16, :] = jnp.concatenate([up, down], axis=0).astype(BF)


def place_kernel(at, info_ref, mine_ref, twin_ref, queue_ref, out_ref, new_ref, sem):
    del queue_ref
    owner, core, z = info_ref[2], info_ref[3], info_ref[4]
    cols, rows = twin_ref.shape[0], twin_ref.shape[1]
    width = twin_ref.shape[2]

    def put(ref, base, c):
        row = lax.broadcasted_iota(jnp.int32, (8, width), 0)
        for a in range(rows // 16):
            for b in range(4):
                tiles = []
                for k in range(4):
                    plane = 4 * b + k
                    slot = (z - plane - c * (cols // 2)) & (cols - 1)
                    block = ref[slot, base + 16 * a:base + 16 * a + 16, :].astype(F32)
                    tiles.append((block[:8], block[8:]))
                for v in range(4):
                    t = [tiles[k][v // 2] for k in range(4)]
                    if v % 2 == 0:
                        up = jnp.where(row < 4, t[0], pltpu.roll(t[1], 4, 0))
                        down = jnp.where(row < 4, t[2], pltpu.roll(t[3], 4, 0))
                    else:
                        up = jnp.where(row < 4, pltpu.roll(t[0], 4, 0), t[1])
                        down = jnp.where(row < 4, pltpu.roll(t[2], 4, 0), t[3])
                    chip = 4 * a + v
                    start = (chip * 2 + c) * 64 + 16 * b
                    new_ref[start:start + 16, :] = jnp.concatenate([up, down], axis=0).astype(BF)

    for mine in (0, 1):
        @pl.when((owner == 1) & (core == mine))
        def _():
            put(mine_ref, at, mine)
            put(twin_ref, 0, 1 - mine)

    @pl.when(owner == 1)
    def _():
        copy = pltpu.make_async_copy(new_ref, out_ref, sem)
        copy.start()
        copy.wait()


def local(queries, positions, queue, new_keys, step):
    nq, width = queries.shape
    slab = queue.shape[0]
    nk = new_keys.shape[0]
    nz = lax.axis_size("z")
    srcs = lax.axis_size("x") * lax.axis_size("y")
    scale = 2.0 / math.sqrt(width)
    chip = lax.axis_index(("x", "y"))
    core = lax.axis_index("c")
    z = lax.axis_index("z")
    slab_index = chip * 2 + core
    swap = [(0, 1), (1, 0)]

    message = pl.pallas_call(
        lambda *refs: message_kernel(srcs, *refs),
        out_shape=jax.ShapeDtypeStruct((srcs, ROWS, width), BF),
        in_specs=[VMEM] * 3,
        out_specs=VMEM,
        scratch_shapes=[pltpu.VMEM((ROWS - nq, width), F32)],
        compiler_params=pltpu.CompilerParams(vmem_limit_bytes=56 * MIB),
    )(queries, positions[None], new_keys)
    got = lax.all_to_all(message, ("x", "y"), 0, 0)
    kept = pl.pallas_call(
        slab_kernel,
        out_shape=jax.ShapeDtypeStruct(queue.shape, BF),
        in_specs=[ANY, VMEM],
        out_specs=ANY,
        scratch_shapes=[pltpu.SemaphoreType.DMA],
        compiler_params=pltpu.CompilerParams(vmem_limit_bytes=56 * MIB),
        cost_estimate=LATE,
    )(message, queue)
    slab_keys, kept = lax.optimization_barrier((queue, kept))
    other = lax.ppermute(slab_keys, "c", swap)

    plane_keys = pl.pallas_call(
        lambda *refs: plane_keys_kernel(nq, *refs),
        out_shape=jax.ShapeDtypeStruct((srcs * nk, width), BF),
        in_specs=[VMEM],
        out_specs=VMEM,
        compiler_params=pltpu.CompilerParams(vmem_limit_bytes=4 * MIB),
        cost_estimate=EARLY,
    )(got)
    pairs = []
    for s in range(srcs):
        for c in range(2):
            for k in range(nz):
                to = (k + s + c * nz // 2) % nz
                pairs.append(((s * 2 + c) * nz + k, (s * 2 + c) * nz + to))
    moved = lax.ppermute(plane_keys, ("x", "y", "c", "z"), pairs)

    owner = (step[0] % (srcs * 2)) == slab_index
    info = jnp.stack([slab_index * slab, (slab_index ^ 1) * slab, owner.astype(jnp.int32), core, z]).astype(jnp.int32)
    n = srcs * nq
    at = 2 * nq
    flops = 2 * n * 2 * slab * width
    out_shape = jax.ShapeDtypeStruct((srcs, at + srcs * nk + 8, width), BF)
    out = pl.pallas_call(
        lambda *refs: partial_kernel(scale, srcs, nq, *refs),
        out_shape=out_shape,
        in_specs=[SMEM, VMEM, VMEM, VMEM, ANY],
        out_specs=VMEM,
        scratch_shapes=[pltpu.VMEM((n, width), BF), pltpu.VMEM((n, 2 * slab), F32)],
        compiler_params=pltpu.CompilerParams(vmem_limit_bytes=24 * MIB),
        cost_estimate=pl.CostEstimate(flops=3 * flops, bytes_accessed=4 * slab * width, transcendentals=2 * n * slab),
    )(info, got, queue, other, plane_keys)
    out = pl.pallas_call(
        lambda *refs: fill_kernel(srcs, at, *refs),
        out_shape=out_shape,
        in_specs=[VMEM, VMEM],
        out_specs=VMEM,
        input_output_aliases={1: 0},
        compiler_params=pltpu.CompilerParams(vmem_limit_bytes=8 * MIB),
    )(moved, out)
    back = lax.all_to_all(out, ("x", "y"), 0, 0)
    twin = lax.ppermute(back[:, at:at + srcs * nk, :], "c", swap)

    loss, grad = pl.pallas_call(
        lambda *refs: combine_kernel(scale, srcs, nq, *refs),
        out_shape=(jax.ShapeDtypeStruct((1, nq), F32), jax.ShapeDtypeStruct((nq, width), BF)),
        in_specs=[VMEM, VMEM],
        out_specs=(VMEM, VMEM),
        compiler_params=pltpu.CompilerParams(vmem_limit_bytes=8 * MIB),
    )(back, queries)
    losses = loss.reshape(nq)

    updated = pl.pallas_call(
        lambda *refs: place_kernel(at, *refs),
        out_shape=jax.ShapeDtypeStruct(queue.shape, BF),
        in_specs=[SMEM, VMEM, VMEM, ANY],
        out_specs=ANY,
        scratch_shapes=[pltpu.VMEM(queue.shape, BF), pltpu.SemaphoreType.DMA],
        input_output_aliases={3: 0},
        compiler_params=pltpu.CompilerParams(vmem_limit_bytes=12 * MIB),
    )(info, back, twin, kept)
    return losses, grad, updated


def solution(mesh):
    gx, gy = mesh.devices.shape
    side = math.isqrt(gx // 2)
    fine = Mesh(np.asarray(mesh.devices).reshape(side, side, 2, gy), ("x", "y", "c", "z"))
    every = ("x", "y", "c", "z")
    return jax.shard_map(
        local,
        mesh=fine,
        in_specs=(P(every, None), P(every), P(("x", "y", "c"), None), P(every, None), P()),
        out_specs=(P(every), P(every, None), P(("x", "y", "c"), None)),
        check_vma=False,
    )
```

```python
import math

import jax
import jax.numpy as jnp
import numpy as np
from jax import lax
from jax.experimental import pallas as pl
from jax.experimental.pallas import tpu as pltpu
from jax.sharding import Mesh, PartitionSpec as P

BF = jnp.bfloat16
F32 = jnp.float32
ROWS = 40
MIB = 1024 * 1024
LOG2E = 1.4426950408889634
VMEM = pl.BlockSpec(memory_space=pltpu.VMEM)
ANY = pl.BlockSpec(memory_space=pl.ANY)
LATE = pl.CostEstimate(flops=6 * 10**9, bytes_accessed=0, transcendentals=0)
EARLY = pl.CostEstimate(flops=92 * 10**8, bytes_accessed=0, transcendentals=0)
SMEM = pl.BlockSpec(memory_space=pltpu.SMEM)


def rows_dot(a, b):
    return lax.dot_general(a, b, (((1,), (1,)), ((), ())), preferred_element_type=F32)


def partial_kernel(scale, srcs, nq, info_ref, msg_ref, own_ref, *refs):
    other_ref, _, _, out_ref, q_ref, s_ref = refs
    width = own_ref.shape[1]
    slab = own_ref.shape[0]
    n = srcs * nq
    block = 256
    lane = lax.broadcasted_iota(jnp.int32, (nq, width), 1)
    row = lax.broadcasted_iota(jnp.int32, (nq, width), 0)
    parts = []
    for j in range(srcs):
        q_ref[j * nq:(j + 1) * nq, :] = msg_ref[j, :nq, :]
        tail = msg_ref[j, nq:, :].astype(F32)
        line = tail[4:5, :] * 256.0 + tail[5:6, :]
        parts.append(jnp.sum(jnp.where(lane == row, line, 0.0), axis=1, keepdims=True))
    target = jnp.concatenate(parts, axis=0).astype(jnp.int32)
    blocks = []
    for b in range(slab // block):
        blocks.append((info_ref[0] + b * block, own_ref, b))
    for b in range(slab // block):
        blocks.append((info_ref[1] + b * block, other_ref, b))
    half = n // 2
    column = lax.broadcasted_iota(jnp.int32, (half, block), 1).astype(F32).astype(BF)
    zero, one = jnp.zeros((half, block), BF), jnp.ones((half, block), BF)

    def score(at, i, top):
        _, ref, b = blocks[i]
        s = rows_dot(q_ref[at, :], ref[b * block:(b + 1) * block, :])
        s_ref[at, i * block:(i + 1) * block] = s
        for c in range(block // 128):
            piece = s[:, c * 128:(c + 1) * 128]
            top = piece if top is None else jnp.maximum(top, piece)
        return top

    halves = (slice(0, half), slice(half, n))
    tops = [None, None]
    for i in range(len(blocks)):
        tops[0] = score(halves[0], i, tops[0])
    found = []
    for h, at in enumerate(halves):
        point = jnp.max(tops[h], axis=1, keepdims=True).astype(BF).astype(F32)
        total = jnp.zeros((half, 128), F32)
        grad = jnp.zeros((half, width), F32)
        positive = jnp.zeros((half, width), F32)
        for i, (start, ref, b) in enumerate(blocks):
            if h == 0:
                tops[1] = score(halves[1], i, tops[1])
            s = s_ref[at, i * block:(i + 1) * block]
            e = jnp.exp2((s - point) * (scale * LOG2E))
            for c in range(block // 128):
                total += e[:, c * 128:(c + 1) * 128]
            hit = column == jnp.broadcast_to((target[at] - start).astype(F32), (half, block)).astype(BF)
            keys = ref[b * block:(b + 1) * block, :]
            grad += jnp.dot(jnp.where(hit, zero, e.astype(BF)), keys, preferred_element_type=F32)
            positive += jnp.dot(jnp.where(hit, one, zero), keys, preferred_element_type=F32)
        found.append((point, total, grad, positive))
    point, total, grad, positive = (jnp.concatenate(pair, axis=0) for pair in zip(*found))
    total = jnp.sum(total, axis=1, keepdims=True)
    t0 = total.astype(BF).astype(F32)
    t1 = (total - t0).astype(BF).astype(F32)
    t2 = total - t0 - t1
    stats = (point, t0, t1, t2)
    grad = grad.astype(BF)
    positive = positive.astype(BF)
    for j in range(srcs):
        at = slice(j * nq, (j + 1) * nq)
        out_ref[j, :nq, :] = grad[at]
        out_ref[j, nq:2 * nq, :] = positive[at]
    lane = lax.broadcasted_iota(jnp.int32, (nq, width), 1)
    row = lax.broadcasted_iota(jnp.int32, (nq, width), 0)
    for j in range(srcs):
        at = slice(j * nq, (j + 1) * nq)
        line = jnp.zeros((nq, width), F32)
        for k, value in enumerate(stats):
            line = jnp.where(lane == row + k * nq, value[at], line)
        line = jnp.sum(line, axis=0, keepdims=True)
        out_ref[j, out_ref.shape[1] - 8:, :] = jnp.broadcast_to(line, (8, width)).astype(BF)


def combine_kernel(scale, srcs, nq, got_ref, q_ref, loss_ref, grad_ref):
    width = q_ref.shape[1]
    lane = lax.broadcasted_iota(jnp.int32, (nq, 128), 1)
    row = lax.broadcasted_iota(jnp.int32, (nq, 128), 0)
    positive = jnp.zeros((nq, width), F32)
    points, totals = [], []
    for j in range(srcs):
        positive += got_ref[j, nq:2 * nq, :].astype(F32)
        st = jnp.broadcast_to(got_ref[j, got_ref.shape[1] - 8:, :].astype(F32)[:1, :128], (nq, 128))
        points.append(jnp.sum(jnp.where(lane == row, st, 0.0), axis=1, keepdims=True))
        three = (lane >= nq) & (lane % nq == row)
        totals.append(jnp.sum(jnp.where(three, st, 0.0), axis=1, keepdims=True))
    s_pos = rows_dot(q_ref[...], positive.astype(BF))
    square = lax.broadcasted_iota(jnp.int32, (nq, nq), 0) == lax.broadcasted_iota(jnp.int32, (nq, nq), 1)
    s_pos = jnp.sum(jnp.where(square, s_pos, 0.0), axis=1, keepdims=True)
    top = s_pos
    for p in points:
        top = jnp.maximum(top, p)
    total = jnp.zeros((nq, 1), F32)
    grad = jnp.zeros((nq, width), F32)
    for j in range(srcs):
        a = jnp.exp2((points[j] - top) * (scale * LOG2E))
        total += a * totals[j]
        grad += a * got_ref[j, :nq, :].astype(F32)
    log_total = jnp.log(total)
    lse = top * scale + log_total
    weight = (jnp.exp(s_pos * scale - lse) - 1.0).astype(BF).astype(F32)
    grad_ref[...] = ((grad / total + weight * positive) * scale).astype(BF)
    loss = lse - s_pos * scale
    loss_ref[...] = jnp.sum(jnp.where(lane == row, loss, 0.0), axis=0, keepdims=True)[:, :nq]


def message_kernel(copies, q_ref, pos_ref, keys_ref, out_ref, tail_ref):
    nq, nk = q_ref.shape[0], keys_ref.shape[0]
    tail_ref[...] = jnp.zeros_like(tail_ref)
    tail_ref[:nk, :] = keys_ref[...].astype(F32)
    tail_ref[nk:nk + 1, :nq] = (pos_ref[...] >> 8).astype(F32)
    tail_ref[nk + 1:nk + 2, :nq] = (pos_ref[...] & 255).astype(F32)
    tail = tail_ref[...].astype(BF)
    for j in range(copies):
        out_ref[j, :nq, :] = q_ref[...]
        out_ref[j, nq:, :] = tail


def fill_kernel(copies, at, keys_ref, in_ref, out_ref):
    del in_ref
    keys = keys_ref[...]
    for j in range(copies):
        out_ref[j, at:at + keys.shape[0], :] = keys


def gate_kernel(after_ref, out_ref):
    del after_ref
    out_ref[...] = jnp.zeros_like(out_ref)


def slab_kernel(after_ref, queue_ref, out_ref, sem):
    del after_ref
    copy = pltpu.make_async_copy(queue_ref, out_ref, sem)
    copy.start()
    copy.wait()


def plane_keys_kernel(nq, got_ref, out_ref):
    width = out_ref.shape[1]
    row = lax.broadcasted_iota(jnp.int32, (8, width), 0)
    for a in range(got_ref.shape[0] // 4):
        t = [got_ref[4 * a + k, nq:, :].astype(F32)[:8] for k in range(4)]
        up = jnp.where(row < 4, t[0], pltpu.roll(t[1], 4, 0))
        down = jnp.where(row < 4, t[2], pltpu.roll(t[3], 4, 0))
        out_ref[16 * a:16 * a + 16, :] = jnp.concatenate([up, down], axis=0).astype(BF)


def place_kernel(at, info_ref, mine_ref, twin_ref, queue_ref, out_ref, new_ref, sem):
    del queue_ref
    owner, core, z = info_ref[2], info_ref[3], info_ref[4]
    cols, rows = twin_ref.shape[0], twin_ref.shape[1]
    width = twin_ref.shape[2]

    def put(ref, base, c):
        row = lax.broadcasted_iota(jnp.int32, (8, width), 0)
        for a in range(rows // 16):
            for b in range(4):
                tiles = []
                for k in range(4):
                    plane = 4 * b + k
                    slot = (z - plane - c * (cols // 2)) & (cols - 1)
                    block = ref[slot, base + 16 * a:base + 16 * a + 16, :].astype(F32)
                    tiles.append((block[:8], block[8:]))
                for v in range(4):
                    t = [tiles[k][v // 2] for k in range(4)]
                    if v % 2 == 0:
                        up = jnp.where(row < 4, t[0], pltpu.roll(t[1], 4, 0))
                        down = jnp.where(row < 4, t[2], pltpu.roll(t[3], 4, 0))
                    else:
                        up = jnp.where(row < 4, pltpu.roll(t[0], 4, 0), t[1])
                        down = jnp.where(row < 4, pltpu.roll(t[2], 4, 0), t[3])
                    chip = 4 * a + v
                    start = (chip * 2 + c) * 64 + 16 * b
                    new_ref[start:start + 16, :] = jnp.concatenate([up, down], axis=0).astype(BF)

    for mine in (0, 1):
        @pl.when((owner == 1) & (core == mine))
        def _():
            put(mine_ref, at, mine)
            put(twin_ref, 0, 1 - mine)

    @pl.when(owner == 1)
    def _():
        copy = pltpu.make_async_copy(new_ref, out_ref, sem)
        copy.start()
        copy.wait()


def local(queries, positions, queue, new_keys, step):
    nq, width = queries.shape
    slab = queue.shape[0]
    nk = new_keys.shape[0]
    nz = lax.axis_size("z")
    srcs = lax.axis_size("x") * lax.axis_size("y")
    scale = 2.0 / math.sqrt(width)
    chip = lax.axis_index(("x", "y"))
    core = lax.axis_index("c")
    z = lax.axis_index("z")
    slab_index = chip * 2 + core
    swap = [(0, 1), (1, 0)]

    message = pl.pallas_call(
        lambda *refs: message_kernel(srcs, *refs),
        out_shape=jax.ShapeDtypeStruct((srcs, ROWS, width), BF),
        in_specs=[VMEM] * 3,
        out_specs=VMEM,
        scratch_shapes=[pltpu.VMEM((ROWS - nq, width), F32)],
        compiler_params=pltpu.CompilerParams(vmem_limit_bytes=56 * MIB),
    )(queries, positions[None], new_keys)
    got = lax.all_to_all(message, ("x", "y"), 0, 0)
    gate = pl.pallas_call(
        gate_kernel,
        out_shape=jax.ShapeDtypeStruct((8, 128), F32),
        in_specs=[ANY],
        out_specs=VMEM,
        compiler_params=pltpu.CompilerParams(vmem_limit_bytes=56 * MIB),
        cost_estimate=LATE,
    )(message)
    slab_keys, gate = lax.optimization_barrier((queue, gate))
    other = lax.ppermute(slab_keys, "c", swap)
    kept = pl.pallas_call(
        slab_kernel,
        out_shape=jax.ShapeDtypeStruct(queue.shape, BF),
        in_specs=[ANY, VMEM],
        out_specs=ANY,
        scratch_shapes=[pltpu.SemaphoreType.DMA],
        compiler_params=pltpu.CompilerParams(vmem_limit_bytes=56 * MIB),
        cost_estimate=LATE,
    )(gate, queue)

    plane_keys = pl.pallas_call(
        lambda *refs: plane_keys_kernel(nq, *refs),
        out_shape=jax.ShapeDtypeStruct((srcs * nk, width), BF),
        in_specs=[VMEM],
        out_specs=VMEM,
        compiler_params=pltpu.CompilerParams(vmem_limit_bytes=4 * MIB),
        cost_estimate=EARLY,
    )(got)
    pairs = []
    for s in range(srcs):
        for c in range(2):
            for k in range(nz):
                to = (k + s + c * nz // 2) % nz
                pairs.append(((s * 2 + c) * nz + k, (s * 2 + c) * nz + to))
    moved = lax.ppermute(plane_keys, ("x", "y", "c", "z"), pairs)

    owner = (step[0] % (srcs * 2)) == slab_index
    info = jnp.stack([slab_index * slab, (slab_index ^ 1) * slab, owner.astype(jnp.int32), core, z]).astype(jnp.int32)
    n = srcs * nq
    at = 2 * nq
    flops = 2 * n * 2 * slab * width
    out_shape = jax.ShapeDtypeStruct((srcs, at + srcs * nk + 8, width), BF)
    out = pl.pallas_call(
        lambda *refs: partial_kernel(scale, srcs, nq, *refs),
        out_shape=out_shape,
        in_specs=[SMEM, VMEM, VMEM, VMEM, ANY, ANY],
        out_specs=VMEM,
        scratch_shapes=[pltpu.VMEM((n, width), BF), pltpu.VMEM((n, 2 * slab), F32)],
        compiler_params=pltpu.CompilerParams(vmem_limit_bytes=24 * MIB),
        cost_estimate=pl.CostEstimate(flops=3 * flops, bytes_accessed=4 * slab * width, transcendentals=2 * n * slab),
    )(info, got, queue, other, plane_keys, kept)
    out = pl.pallas_call(
        lambda *refs: fill_kernel(srcs, at, *refs),
        out_shape=out_shape,
        in_specs=[VMEM, VMEM],
        out_specs=VMEM,
        input_output_aliases={1: 0},
        compiler_params=pltpu.CompilerParams(vmem_limit_bytes=8 * MIB),
    )(moved, out)
    back = lax.all_to_all(out, ("x", "y"), 0, 0)
    twin = lax.ppermute(back[:, at:at + srcs * nk, :], "c", swap)

    loss, grad = pl.pallas_call(
        lambda *refs: combine_kernel(scale, srcs, nq, *refs),
        out_shape=(jax.ShapeDtypeStruct((1, nq), F32), jax.ShapeDtypeStruct((nq, width), BF)),
        in_specs=[VMEM, VMEM],
        out_specs=(VMEM, VMEM),
        compiler_params=pltpu.CompilerParams(vmem_limit_bytes=8 * MIB),
    )(back, queries)
    losses = loss.reshape(nq)

    updated = pl.pallas_call(
        lambda *refs: place_kernel(at, *refs),
        out_shape=jax.ShapeDtypeStruct(queue.shape, BF),
        in_specs=[SMEM, VMEM, VMEM, ANY],
        out_specs=ANY,
        scratch_shapes=[pltpu.VMEM(queue.shape, BF), pltpu.SemaphoreType.DMA],
        input_output_aliases={3: 0},
        compiler_params=pltpu.CompilerParams(vmem_limit_bytes=12 * MIB),
    )(info, back, twin, kept)
    return losses, grad, updated


def solution(mesh):
    gx, gy = mesh.devices.shape
    side = math.isqrt(gx // 2)
    fine = Mesh(np.asarray(mesh.devices).reshape(side, side, 2, gy), ("x", "y", "c", "z"))
    every = ("x", "y", "c", "z")
    return jax.shard_map(
        local,
        mesh=fine,
        in_specs=(P(every, None), P(every), P(("x", "y", "c"), None), P(every, None), P()),
        out_specs=(P(every), P(every, None), P(("x", "y", "c"), None)),
        check_vma=False,
    )
```
